32 devices in a mesh: groups: 2 (over y), gx: 4 (over z), gy: 2 (over x), gz: 2 (over core).
Axes of the slice: x: 2, y: 2, z: 4, core: 2. Of those that a mesh axis runs over, the one named last changes fastest.
Arguments:
- tokens: bfloat16 [128, 18432], P(('groups', 'gy', 'gz'), 'gx'), parts along dimension 0, may hold values from -6 to 6
- q_weight: bfloat16 [18432, 6144], P('gx', ('gy', 'gz')), may hold values from -0.046875 to 0.046875
- o_weight: bfloat16 [6144, 18432], P(('gy', 'gz'), 'gx'), may hold values from -0.078125 to 0.078125
- key_cache: bfloat16 [128, 512, 256], P(('groups', 'gx', 'gy', 'gz')), parts along dimension 0, may hold values from -410 to 410
- value_cache: bfloat16 [128, 512, 256], P(('groups', 'gx', 'gy', 'gz')), parts along dimension 0, may hold values from -8 to 8
- lengths: int32 [128], P(('groups', 'gx', 'gy', 'gz')), parts along dimension 0, may hold values from 2 to 512, as said below
Outputs:
- output: bfloat16 [128, 18432], P(('groups', 'gy', 'gz'), 'gx'), parts along dimension 0
The draws below stay inside these ranges and needn't reach their ends.
There are 2 independent parts, one for each index of `groups`. The reference program is written for one: setup_inputs(seed, part) draws one part's arguments, and reference() takes and returns one part's arrays. A program takes and returns all parts, laid end to end along the dimension named above; an argument that names none is the same for every part. Nothing has to cross between parts.
Inputs may be any that keep to these rules, and one draw needn't show every extreme that they name: `lengths`: one row uses all 512 positions.
All inputs are finite; a program needn't handle non-finite values.
Results may differ from the reference program's by a relative error of at most 0.025.
Values may be sent and summed in bfloat16 or wider, within the bound.
No kernel may reach another device: no remote copies, remote signals or barrier semaphores. Data moves between devices by JAX's collectives and lax.ppermute only.
A program may use at most 128 MiB of HBM per device.

```python
import math
import jax
import jax.numpy as jnp
from jax import lax

D = 18432
HEADS = 24
HDIM = 256
CACHE = 512
ROWS = 64
N_GX = 4
N_GY = 2
N_GZ = 2


def draw_key_cache(key, part):
    key = jax.random.fold_in(key, 5)
    key_base = jax.random.fold_in(key, 0)
    drawn = 2.0 * jax.random.truncated_normal(key_base, -4.0, 4.0, (ROWS, CACHE, HDIM), jnp.float32)
    return drawn.astype(jnp.bfloat16)


def draw_lengths(key, part):
    key = jax.random.fold_in(key, 7)
    key_rows, key_pick = jax.random.split(key, 2)
    lengths_drawn = jax.random.randint(key_rows, (ROWS,), 2, CACHE + 1)
    longest = jax.random.randint(key_pick, (), 0, ROWS)
    return jnp.where(jnp.arange(ROWS) == longest, CACHE, lengths_drawn).astype(jnp.int32)


def block_scale(own_key, extent, pieces, least, high):
    loudness = 1.0
    for position, blocks in pieces:
        steps = jax.random.uniform(jax.random.fold_in(jax.random.fold_in(own_key, 6), position), (blocks,), jnp.float32, least / len(pieces), high / len(pieces))
        loudness = loudness * jnp.repeat(jnp.exp(steps), extent[position] // blocks).reshape((-1,) + (1,) * (len(extent) - 1 - position))
    return loudness


def bell_draw(rng, dims, deviation, limit, cuts=(), kind=jnp.bfloat16):
    values = deviation * jax.random.normal(rng, dims, jnp.float32)
    if cuts:
        values = values * block_scale(rng, dims, cuts, -0.22, 0.18)
    return jnp.clip(values, -limit, limit).astype(kind)


def setup_inputs(seed: int = 0, part: int = 0) -> dict:
    key_list = jax.random.split(jax.random.key(seed), 7)
    part_keys = jax.random.split(jax.random.fold_in(key_list[6], part), 7)
    tokens = bell_draw(part_keys[0], (ROWS, D), 1.0, 6.0, ((0, 4), (1, 4)))
    q_weight = bell_draw(key_list[1], (D, HEADS * HDIM), D ** -0.5, 0.046875, ((0, 4), (1, 4)))
    o_weight = bell_draw(key_list[2], (HEADS * HDIM, D), (HEADS * HDIM) ** -0.5, 0.078125, ((0, 4), (1, 4)))
    key_cache = draw_key_cache(jax.random.fold_in(jax.random.fold_in(key_list[6], part), 71), part)
    value_cache = bell_draw(part_keys[4], (ROWS, CACHE, HDIM), 2.0, 8.0, ((0, 16),))
    lengths = draw_lengths(jax.random.fold_in(jax.random.fold_in(key_list[6], part), 71), part)
    return dict(tokens=tokens, q_weight=q_weight, o_weight=o_weight, key_cache=key_cache, value_cache=value_cache, lengths=lengths)


def block_sum(left, right, blocks):
    row_count = left.shape[0]
    block_width = left.shape[1] // blocks
    left_blocks = left.reshape(row_count, blocks, block_width).transpose(1, 0, 2)
    right_blocks = right.reshape(blocks, block_width, right.shape[1])

    def add_term(running, operands):
        product_term = jnp.dot(operands[0], operands[1], preferred_element_type=jnp.float32)
        product_term = lax.optimization_barrier(product_term.astype(jnp.bfloat16)).astype(jnp.float32)
        return running + product_term, None

    start_value = jnp.zeros((row_count, right.shape[1]), jnp.float32)
    summed, _ = lax.scan(add_term, start_value, (left_blocks, right_blocks))
    return summed.astype(jnp.bfloat16)


def attend_group(operands):
    query_block, key_block, value_block, length_block = operands
    row_group = query_block.shape[0]
    query = query_block.reshape(row_group, HEADS, HDIM).astype(jnp.float32)
    scores = jnp.einsum("rhd,rld->rhl", query, key_block.astype(jnp.float32), precision=lax.Precision.HIGHEST) * (HDIM ** -0.5)
    positions = lax.broadcasted_iota(jnp.int32, (row_group, CACHE), 1)
    usable = positions < length_block[:, None]
    scores = jnp.where(usable[:, None, :], scores, -jnp.inf)
    largest = jnp.max(scores, axis=2, keepdims=True)
    raised = jnp.exp(scores - largest)
    totals = jnp.sum(raised, axis=2, keepdims=True)
    weights = (raised / totals).astype(jnp.bfloat16)
    mixed = jnp.einsum("rhl,rld->rhd", weights.astype(jnp.float32), value_block.astype(jnp.float32), precision=lax.Precision.HIGHEST)
    return mixed.astype(jnp.bfloat16).reshape(row_group, HEADS * HDIM)


def reference(tokens, q_weight, o_weight, key_cache, value_cache, lengths):
    queries = block_sum(tokens, q_weight, N_GX)
    row_group = math.gcd(ROWS, 64)
    groups_count = ROWS // row_group
    mixed = lax.map(attend_group, (
        queries.reshape(groups_count, row_group, HEADS * HDIM),
        key_cache.reshape(groups_count, row_group, CACHE, HDIM),
        value_cache.reshape(groups_count, row_group, CACHE, HDIM),
        lengths.reshape(groups_count, row_group)))
    mixed = mixed.reshape(ROWS, HEADS * HDIM)
    return block_sum(mixed, o_weight, N_GY * N_GZ)
```

```python
import functools

import jax
import jax.numpy as jnp
from jax import lax
from jax.experimental import pallas as pl
from jax.experimental.pallas import tpu as pltpu
from jax.sharding import PartitionSpec as P

HDIM = 256
BF16 = jnp.bfloat16
F32 = jnp.float32
VMEM = pl.BlockSpec(memory_space=pltpu.VMEM)
ANY = pl.BlockSpec(memory_space=pl.ANY)
SMEM = pl.BlockSpec(memory_space=pltpu.SMEM)


def shift(array, axis, by):
    size = lax.axis_size(axis)
    return lax.ppermute(array, axis, [(s, (s + by) % size) for s in range(size)])


def largest_divisor(extent, limit, unit):
    best = extent
    for size in range(unit, limit + 1, unit):
        if extent % size == 0:
            best = size
    return best


def call(body, outs, operands, in_specs, scratch=(), mib=8, flops=0, name=None):
    moved = sum(a.size * a.dtype.itemsize for a in operands)
    moved += sum(o.size * o.dtype.itemsize for o in outs)
    return pl.pallas_call(
        body,
        out_shape=list(outs),
        in_specs=in_specs,
        out_specs=[VMEM] * len(outs),
        scratch_shapes=list(scratch),
        compiler_params=pltpu.CompilerParams(vmem_limit_bytes=mib * 2**20),
        cost_estimate=pl.CostEstimate(flops=flops, bytes_accessed=moved, transcendentals=0),
        name=name,
    )(*operands)


def query_body(n_gx, n_gy, n_gz, chunk, where, *refs):
    count = n_gy * n_gz
    pieces, weight = refs[:count], refs[count]
    outs = refs[count + 1 : count + 1 + n_gx]
    rows, total, held, sems = refs[count + 1 + n_gx :]
    chunks = weight.shape[0] // chunk

    def copy(c):
        span = pl.ds(c * chunk, chunk)
        return pltpu.make_async_copy(weight.at[span, :], held.at[span, :], sems.at[c])

    for c in range(chunks):
        copy(c).start()
    block = pieces[0].shape[0]
    for k in range(n_gy):
        for j in range(n_gz):
            at = lax.rem(where[1] + n_gy - k, n_gy) * n_gz + lax.rem(where[2] + n_gz - j, n_gz)
            rows[pl.ds(pl.multiple_of(at * block, block), block), :] = pieces[k * n_gz + j][...]
    for c in range(chunks):
        copy(c).wait()
        span = slice(c * chunk, (c + 1) * chunk)
        term = jnp.dot(rows[:, span], held[span, :], preferred_element_type=F32)
        if c == 0:
            total[...] = term
        else:
            total[...] += term
    part = outs[0].shape[0]
    for k in range(n_gx):
        at = pl.multiple_of(lax.rem(where[0] + k, n_gx) * part, part)
        outs[k][...] = total[pl.ds(at, part), :].astype(BF16)


def sum_split_body(n_gx, n_gy, n_gz, where, *refs):
    pieces, outs, total = refs[:n_gx], refs[n_gx : n_gx + n_gy], refs[-1]
    value = pieces[0][...].astype(F32)
    for piece in pieces[1:]:
        value = value + piece[...].astype(F32)
    each = outs[0].shape[1]
    for at in range(n_gy * n_gz):
        total[at] = value[at * each : (at + 1) * each]
    for k in range(n_gy):
        for j in range(n_gz):
            outs[k][j] = total[lax.rem(where[1] + k, n_gy) * n_gz + j].astype(BF16)


def attend_body(n_gy, n_gz, where, lengths, *refs):
    count = n_gy * n_gz
    pieces, key, value, outs = refs[:count], refs[count], refs[count + 1], refs[count + 2 :]
    each, width = pieces[0].shape[1:]
    heads = width // HDIM
    stacked = []
    for piece in pieces:
        mine = piece[where[2]].astype(F32)
        stacked += [mine[:, h * HDIM : (h + 1) * HDIM] for h in range(heads)]
    query = jnp.concatenate(stacked, axis=0).astype(BF16)
    cache = key.shape[1]
    keys = key[...].reshape(each * cache, HDIM)
    values = value[...].reshape(each * cache, HDIM)
    scores = lax.dot_general(query, keys, (((1,), (1,)), ((), ())), preferred_element_type=F32)
    scores = scores * HDIM ** (-0.5)
    row = lax.rem(lax.broadcasted_iota(jnp.int32, scores.shape, 0), each)
    place = lax.broadcasted_iota(jnp.int32, scores.shape, 1) - row * cache
    used = jnp.zeros((scores.shape[0], 1), jnp.int32)
    row_of = lax.rem(lax.broadcasted_iota(jnp.int32, (scores.shape[0], 1), 0), each)
    for r in range(each):
        used = jnp.where(row_of == r, lengths[r], used)
    scores = jnp.where((place >= 0) & (place < used), scores, -jnp.inf)
    raised = jnp.exp(scores - jnp.max(scores, axis=1, keepdims=True))
    totals = jnp.sum(raised, axis=1, keepdims=True)
    mixed = jnp.dot(raised.astype(BF16), values, preferred_element_type=F32) / totals
    for k in range(n_gy):
        for j in range(n_gz):
            source = ((n_gy - k) % n_gy) * n_gz + (n_gz - j) % n_gz
            for h in range(heads):
                at = (source * heads + h) * each
                outs[k][j, :, h * HDIM : (h + 1) * HDIM] = mixed[at : at + each].astype(BF16)


def gather_rows_body(n_gy, n_gz, where, *refs):
    pieces, out, total = refs[:-2], refs[-2], refs[-1]
    each = pieces[0].shape[1]
    for k in range(n_gy):
        for j in range(n_gz):
            at = lax.rem(where[1] + n_gy - k, n_gy) * n_gz + lax.rem(where[2] + n_gz - j, n_gz)
            total[at] = pieces[k * n_gz + j][j].astype(F32)
    out[...] = jnp.concatenate([total[i] for i in range(n_gy * n_gz)], axis=0).astype(BF16)


def output_body(n_gx, n_gy, n_gz, chunk, where, *refs):
    pieces, weight = refs[:n_gx], refs[n_gx]
    count = n_gy * n_gz
    outs = refs[n_gx + 1 : n_gx + 1 + count]
    rows, total, held, sems = refs[n_gx + 1 + count :]
    chunks = weight.shape[1] // chunk

    def copy(c):
        span = pl.ds(c * chunk, chunk)
        return pltpu.make_async_copy(weight.at[:, span], held.at[:, span], sems.at[c])

    for c in range(chunks):
        copy(c).start()
    block = pieces[0].shape[0]
    for k in range(n_gx):
        at = pl.multiple_of(lax.rem(where[0] + n_gx - k, n_gx) * block, block)
        rows[pl.ds(at, block), :] = pieces[k][...]
    part = outs[0].shape[0]
    for c in range(chunks):
        copy(c).wait()
        span = slice(c * chunk, (c + 1) * chunk)
        total[...] = jnp.dot(rows[...], held[:, span], preferred_element_type=F32)
        for k in range(n_gy):
            for j in range(n_gz):
                at = lax.rem(where[1] + k, n_gy) * n_gz + lax.rem(where[2] + j, n_gz)
                at = pl.multiple_of(at * part, part)
                outs[k * n_gz + j][:, span] = total[pl.ds(at, part), :].astype(BF16)


def sum_body(*refs):
    value = refs[0][...].astype(F32)
    for ref in refs[1:-1]:
        value = value + ref[...].astype(F32)
    refs[-1][...] = value.astype(BF16)


def added(arrays, name):
    out = jax.ShapeDtypeStruct(arrays[0].shape, BF16)
    return call(sum_body, [out], arrays, [VMEM] * len(arrays), name=name)[0]


def mib_for(*sizes):
    return max(8, -(-int(sum(sizes) * 1.25) // 2**20) + 2)


def shards(tokens, q_weight, o_weight, key_cache, value_cache, lengths):
    n_gx, n_gy, n_gz = (lax.axis_size(a) for a in ("gx", "gy", "gz"))
    where = jnp.stack([lax.axis_index(a) for a in ("gx", "gy", "gz")]).astype(jnp.int32)
    own_rows, depth = tokens.shape
    row_count = own_rows * n_gy * n_gz
    width = q_weight.shape[1]
    each = key_cache.shape[0]
    part = row_count // n_gx
    struct = jax.ShapeDtypeStruct

    pieces = []
    for k in range(n_gy):
        over = shift(tokens, "gy", k) if k else tokens
        pieces += [shift(over, "gz", j) if j else over for j in range(n_gz)]
    chunk = largest_divisor(depth, 512, 128)
    terms = call(
        functools.partial(query_body, n_gx, n_gy, n_gz, chunk),
        [struct((part, width), BF16)] * n_gx,
        [where, *pieces, q_weight],
        [SMEM] + [VMEM] * len(pieces) + [ANY],
        scratch=[
            pltpu.VMEM((row_count, depth), BF16),
            pltpu.VMEM((row_count, width), F32),
            pltpu.VMEM(q_weight.shape, BF16),
            pltpu.SemaphoreType.DMA((depth // chunk,)),
        ],
        mib=mib_for(row_count * depth * 4, row_count * width * 8, depth * width * 2),
        flops=2 * row_count * depth * width,
        name="query_terms",
    )

    terms = [terms[0]] + [shift(terms[k], "gx", k) for k in range(1, n_gx)]
    queries = call(
        functools.partial(sum_split_body, n_gx, n_gy, n_gz),
        [struct((n_gz, each, width), BF16)] * n_gy,
        [where, *terms],
        [SMEM] + [VMEM] * n_gx,
        scratch=[pltpu.VMEM((n_gy * n_gz, each, width), F32)],
        name="query_sum",
    )
    pieces = []
    for k in range(n_gy):
        over = shift(queries[k], "gy", k) if k else queries[k]
        pieces += [shift(over, "gz", j) if j else over for j in range(n_gz)]
    mixed = call(
        functools.partial(attend_body, n_gy, n_gz),
        [struct((n_gz, each, width), BF16)] * n_gy,
        [where, lengths, *pieces, key_cache, value_cache],
        [SMEM, SMEM] + [VMEM] * (len(pieces) + 2),
        mib=24,
        name="attention",
    )

    pieces = []
    for k in range(n_gy):
        over = shift(mixed[k], "gy", k) if k else mixed[k]
        pieces += [shift(over, "gz", j) if j else over for j in range(n_gz)]
    block = call(
        functools.partial(gather_rows_body, n_gy, n_gz),
        [struct((part, width), BF16)],
        [where, *pieces],
        [SMEM] + [VMEM] * len(pieces),
        scratch=[pltpu.VMEM((n_gy * n_gz, each, width), F32)],
        name="mixed_rows",
    )[0]
    blocks = [block] + [shift(block, "gx", k) for k in range(1, n_gx)]
    columns = o_weight.shape[1]
    chunk = largest_divisor(columns, 512, 128)
    terms = call(
        functools.partial(output_body, n_gx, n_gy, n_gz, chunk),
        [struct((own_rows, columns), BF16)] * (n_gy * n_gz),
        [where, *blocks, o_weight],
        [SMEM] + [VMEM] * n_gx + [ANY],
        scratch=[
            pltpu.VMEM((row_count, width), BF16),
            pltpu.VMEM((row_count, chunk), F32),
            pltpu.VMEM(o_weight.shape, BF16),
            pltpu.SemaphoreType.DMA((columns // chunk,)),
        ],
        mib=mib_for(row_count * width * 4, row_count * (chunk * 4 + columns * 2), columns * width * 2),
        flops=2 * row_count * columns * width,
        name="output_terms",
    )

    arrived = []
    for k in range(1, n_gy):
        mine = terms[k * n_gz : (k + 1) * n_gz]
        mine = [mine[0]] + [shift(mine[j], "gz", j) for j in range(1, n_gz)]
        arrived.append(shift(added(mine, "pair_sum") if n_gz > 1 else mine[0], "gy", k))
    mine = [terms[0]] + [shift(terms[j], "gz", j) for j in range(1, n_gz)]
    return added(mine + arrived, "output_sum")


def solution(mesh):
    return jax.shard_map(
        shards,
        mesh=mesh,
        in_specs=(
            P(("groups", "gy", "gz"), "gx"),
            P("gx", ("gy", "gz")),
            P(("gy", "gz"), "gx"),
            P(("groups", "gx", "gy", "gz"), None, None),
            P(("groups", "gx", "gy", "gz"), None, None),
            P(("groups", "gx", "gy", "gz")),
        ),
        out_specs=P(("groups", "gy", "gz"), "gx"),
        check_vma=False,
    )
```

```python
import functools

import jax
import jax.numpy as jnp
from jax import lax
from jax.experimental import pallas as pl
from jax.experimental.pallas import tpu as pltpu
from jax.sharding import PartitionSpec as P

HDIM = 256
BF16 = jnp.bfloat16
F32 = jnp.float32
VMEM = pl.BlockSpec(memory_space=pltpu.VMEM)
ANY = pl.BlockSpec(memory_space=pl.ANY)
SMEM = pl.BlockSpec(memory_space=pltpu.SMEM)


def shift(array, axis, by):
    size = lax.axis_size(axis)
    return lax.ppermute(array, axis, [(s, (s + by) % size) for s in range(size)])


def position():
    return tuple(lax.axis_index(a) for a in ("gx", "gy", "gz"))


def largest_divisor(extent, limit, unit):
    best = extent
    for size in range(unit, limit + 1, unit):
        if extent % size == 0:
            best = size
    return best


def call(body, outs, operands, in_specs, scratch=(), mib=8, flops=0, beside=0, name=None):
    moved = sum(a.size * a.dtype.itemsize for a in operands)
    moved += sum(o.size * o.dtype.itemsize for o in outs)
    return pl.pallas_call(
        body,
        out_shape=list(outs),
        in_specs=in_specs,
        out_specs=[VMEM] * len(outs),
        scratch_shapes=list(scratch),
        compiler_params=pltpu.CompilerParams(vmem_limit_bytes=mib * 2**20),
        cost_estimate=pl.CostEstimate(flops=flops + beside, bytes_accessed=moved, transcendentals=0),
        name=name,
    )(*operands)


def stage_body(tokens, out, sem):
    copy = pltpu.make_async_copy(tokens, out, sem)
    copy.start()
    copy.wait()


def query_body(n_gx, n_gy, n_gz, chunk, *refs):
    where = position()
    count = n_gy * n_gz
    pieces, weight = refs[:count], refs[count]
    outs = refs[count + 1 : count + 1 + n_gx]
    rows, total = refs[count + 1 + n_gx :]
    block = pieces[0].shape[0]
    for k in range(n_gy):
        for j in range(n_gz):
            at = lax.rem(where[1] + n_gy - k, n_gy) * n_gz + lax.rem(where[2] + n_gz - j, n_gz)
            rows[pl.ds(pl.multiple_of(at * block, block), block), :] = pieces[k * n_gz + j][...]

    @pl.loop(0, weight.shape[1] // chunk)
    def _(c):
        span = pl.ds(pl.multiple_of(c * chunk, chunk), chunk)
        total[:, span] = jnp.dot(rows[...], weight[:, span], preferred_element_type=F32)

    part = outs[0].shape[0]
    for k in range(n_gx):
        at = pl.multiple_of(lax.rem(where[0] + k, n_gx) * part, part)
        outs[k][...] = total[pl.ds(at, part), :].astype(BF16)


def sum_split_body(n_gx, n_gy, n_gz, *refs):
    where = position()
    pieces, outs, total = refs[:n_gx], refs[n_gx : n_gx + n_gy], refs[-1]
    value = pieces[0][...].astype(F32)
    for piece in pieces[1:]:
        value = value + piece[...].astype(F32)
    each = outs[0].shape[1]
    for at in range(n_gy * n_gz):
        total[at] = value[at * each : (at + 1) * each]
    for k in range(n_gy):
        for j in range(n_gz):
            outs[k][j] = total[lax.rem(where[1] + k, n_gy) * n_gz + j].astype(BF16)


def attend_body(n_gy, n_gz, lengths, *refs):
    where = position()
    count = n_gy * n_gz
    pieces, key, value, outs = refs[:count], refs[count], refs[count + 1], refs[count + 2 :]
    each, width = pieces[0].shape[1:]
    heads = width // HDIM
    stacked = []
    for piece in pieces:
        mine = piece[where[2]].astype(F32)
        stacked += [mine[:, h * HDIM : (h + 1) * HDIM] for h in range(heads)]
    query = jnp.concatenate(stacked, axis=0).astype(BF16)
    cache = key.shape[1]
    keys = key[...].reshape(each * cache, HDIM)
    values = value[...].reshape(each * cache, HDIM)
    scores = lax.dot_general(query, keys, (((1,), (1,)), ((), ())), preferred_element_type=F32)
    scores = scores * HDIM ** (-0.5)
    row = lax.rem(lax.broadcasted_iota(jnp.int32, scores.shape, 0), each)
    place = lax.broadcasted_iota(jnp.int32, scores.shape, 1) - row * cache
    used = jnp.zeros((scores.shape[0], 1), jnp.int32)
    row_of = lax.rem(lax.broadcasted_iota(jnp.int32, (scores.shape[0], 1), 0), each)
    for r in range(each):
        used = jnp.where(row_of == r, lengths[r], used)
    scores = jnp.where((place >= 0) & (place < used), scores, -jnp.inf)
    raised = jnp.exp(scores - jnp.max(scores, axis=1, keepdims=True))
    totals = jnp.sum(raised, axis=1, keepdims=True)
    mixed = jnp.dot(raised.astype(BF16), values, preferred_element_type=F32) / totals
    for k in range(n_gy):
        for j in range(n_gz):
            source = ((n_gy - k) % n_gy) * n_gz + (n_gz - j) % n_gz
            for h in range(heads):
                at = (source * heads + h) * each
                outs[k][j, :, h * HDIM : (h + 1) * HDIM] = mixed[at : at + each].astype(BF16)


def gather_rows_body(n_gy, n_gz, *refs):
    where = position()
    pieces, out, total = refs[:-2], refs[-2], refs[-1]
    each = pieces[0].shape[1]
    for k in range(n_gy):
        for j in range(n_gz):
            at = lax.rem(where[1] + n_gy - k, n_gy) * n_gz + lax.rem(where[2] + n_gz - j, n_gz)
            total[at] = pieces[k * n_gz + j][j].astype(F32)
    out[...] = jnp.concatenate([total[i] for i in range(n_gy * n_gz)], axis=0).astype(BF16)


def output_body(n_gx, n_gy, n_gz, chunk, *refs):
    where = position()
    pieces, weight = refs[:n_gx], refs[n_gx]
    count = n_gy * n_gz
    outs = refs[n_gx + 1 : n_gx + 1 + count]
    rows, total = refs[n_gx + 1 + count :]
    block = pieces[0].shape[0]
    for k in range(n_gx):
        at = pl.multiple_of(lax.rem(where[0] + n_gx - k, n_gx) * block, block)
        rows[pl.ds(at, block), :] = pieces[k][...]
    part = outs[0].shape[0]

    @pl.loop(0, weight.shape[1] // chunk)
    def _(c):
        span = pl.ds(pl.multiple_of(c * chunk, chunk), chunk)
        total[...] = jnp.dot(rows[...], weight[:, span], preferred_element_type=F32)
        for k in range(n_gy):
            for j in range(n_gz):
                at = lax.rem(where[1] + k, n_gy) * n_gz + lax.rem(where[2] + j, n_gz)
                at = pl.multiple_of(at * part, part)
                outs[k * n_gz + j][:, span] = total[pl.ds(at, part), :].astype(BF16)


def sum_body(*refs):
    value = refs[0][...].astype(F32)
    for ref in refs[1:-1]:
        value = value + ref[...].astype(F32)
    refs[-1][...] = value.astype(BF16)


def added(arrays, name):
    out = jax.ShapeDtypeStruct(arrays[0].shape, BF16)
    return call(sum_body, [out], arrays, [VMEM] * len(arrays), name=name)[0]


def mib_for(*sizes):
    return max(8, -(-int(sum(sizes) * 1.25) // 2**20) + 2)


def shards(tokens, q_weight, o_weight, key_cache, value_cache, lengths):
    n_gx, n_gy, n_gz = (lax.axis_size(a) for a in ("gx", "gy", "gz"))
    own_rows, depth = tokens.shape
    row_count = own_rows * n_gy * n_gz
    width = q_weight.shape[1]
    each = key_cache.shape[0]
    part = row_count // n_gx
    struct = jax.ShapeDtypeStruct

    weight_bytes = 2 * depth * width
    staged = call(
        stage_body,
        [struct(tokens.shape, BF16)],
        [tokens],
        [ANY],
        scratch=[pltpu.SemaphoreType.DMA],
        beside=3000 * weight_bytes,
        name="own_tokens",
    )[0]
    pieces = []
    for k in range(n_gy):
        over = shift(tokens, "gy", k) if k else tokens
        pieces += [shift(over, "gz", j) if j else over for j in range(n_gz)]
    pieces[0] = staged
    chunk = largest_divisor(width, 256, 128)
    terms = call(
        functools.partial(query_body, n_gx, n_gy, n_gz, chunk),
        [struct((part, width), BF16)] * n_gx,
        [*pieces, q_weight],
        [VMEM] * len(pieces) + [VMEM],
        scratch=[
            pltpu.VMEM((row_count, depth), BF16),
            pltpu.VMEM((row_count, width), F32),
        ],
        mib=mib_for(row_count * depth * 4, row_count * width * 8, depth * width * 2),
        flops=2 * row_count * depth * width,
        name="query_terms",
    )

    terms = [terms[0]] + [shift(terms[k], "gx", k) for k in range(1, n_gx)]
    queries = call(
        functools.partial(sum_split_body, n_gx, n_gy, n_gz),
        [struct((n_gz, each, width), BF16)] * n_gy,
        [*terms],
        [VMEM] * n_gx,
        scratch=[pltpu.VMEM((n_gy * n_gz, each, width), F32)],
        beside=20000 * key_cache.size,
        name="query_sum",
    )
    pieces = []
    for k in range(n_gy):
        over = shift(queries[k], "gy", k) if k else queries[k]
        pieces += [shift(over, "gz", j) if j else over for j in range(n_gz)]
    mixed = call(
        functools.partial(attend_body, n_gy, n_gz),
        [struct((n_gz, each, width), BF16)] * n_gy,
        [lengths, *pieces, key_cache, value_cache],
        [SMEM] + [VMEM] * (len(pieces) + 2),
        mib=12,
        name="attention",
    )

    pieces = []
    for k in range(n_gy):
        over = shift(mixed[k], "gy", k) if k else mixed[k]
        pieces += [shift(over, "gz", j) if j else over for j in range(n_gz)]
    block = call(
        functools.partial(gather_rows_body, n_gy, n_gz),
        [struct((part, width), BF16)],
        [*pieces],
        [VMEM] * len(pieces),
        scratch=[pltpu.VMEM((n_gy * n_gz, each, width), F32)],
        name="mixed_rows",
    )[0]
    blocks = [block] + [shift(block, "gx", k) for k in range(1, n_gx)]
    columns = o_weight.shape[1]
    chunk = largest_divisor(columns, 512, 128)
    terms = call(
        functools.partial(output_body, n_gx, n_gy, n_gz, chunk),
        [struct((own_rows, columns), BF16)] * (n_gy * n_gz),
        [*blocks, o_weight],
        [VMEM] * n_gx + [VMEM],
        scratch=[
            pltpu.VMEM((row_count, width), BF16),
            pltpu.VMEM((row_count, chunk), F32),
        ],
        mib=mib_for(row_count * width * 4, row_count * (chunk * 4 + columns * 2), columns * width * 2),
        flops=2 * row_count * columns * width,
        name="output_terms",
    )

    arrived = []
    for k in range(1, n_gy):
        mine = terms[k * n_gz : (k + 1) * n_gz]
        mine = [mine[0]] + [shift(mine[j], "gz", j) for j in range(1, n_gz)]
        arrived.append(shift(added(mine, "pair_sum") if n_gz > 1 else mine[0], "gy", k))
    mine = [terms[0]] + [shift(terms[j], "gz", j) for j in range(1, n_gz)]
    return added(mine + arrived, "output_sum")


def solution(mesh):
    return jax.shard_map(
        shards,
        mesh=mesh,
        in_specs=(
            P(("groups", "gy", "gz"), "gx"),
            P("gx", ("gy", "gz")),
            P(("gy", "gz"), "gx"),
            P(("groups", "gx", "gy", "gz"), None, None),
            P(("groups", "gx", "gy", "gz"), None, None),
            P(("groups", "gx", "gy", "gz")),
        ),
        out_specs=P(("groups", "gy", "gz"), "gx"),
        check_vma=False,
    )
```

```python
import functools

import jax
import jax.numpy as jnp
from jax import lax
from jax.experimental import pallas as pl
from jax.experimental.pallas import tpu as pltpu
from jax.sharding import PartitionSpec as P

HDIM = 256
BF16 = jnp.bfloat16
F32 = jnp.float32
VMEM = pl.BlockSpec(memory_space=pltpu.VMEM)
ANY = pl.BlockSpec(memory_space=pl.ANY)
SMEM = pl.BlockSpec(memory_space=pltpu.SMEM)


def shift(array, axis, by):
    size = lax.axis_size(axis)
    return lax.ppermute(array, axis, [(s, (s + by) % size) for s in range(size)])


def position():
    return tuple(lax.axis_index(a) for a in ("gx", "gy", "gz"))


def largest_divisor(extent, limit, unit):
    best = extent
    for size in range(unit, limit + 1, unit):
        if extent % size == 0:
            best = size
    return best


def call(body, outs, operands, in_specs, scratch=(), mib=8, flops=0, beside=0, name=None):
    moved = sum(a.size * a.dtype.itemsize for a in operands)
    moved += sum(o.size * o.dtype.itemsize for o in outs)
    return pl.pallas_call(
        body,
        out_shape=list(outs),
        in_specs=in_specs,
        out_specs=[VMEM] * len(outs),
        scratch_shapes=list(scratch),
        compiler_params=pltpu.CompilerParams(vmem_limit_bytes=mib * 2**20),
        cost_estimate=pl.CostEstimate(flops=flops + beside, bytes_accessed=moved, transcendentals=0),
        name=name,
    )(*operands)


def stage_body(tokens, out, sem):
    copy = pltpu.make_async_copy(tokens, out, sem)
    copy.start()
    copy.wait()


def query_body(n_gx, n_gy, n_gz, chunk, *refs):
    where = position()
    count = n_gy * n_gz
    pieces, weight = refs[:count], refs[count]
    outs = refs[count + 1 : count + 1 + n_gx]
    rows, total = refs[count + 1 + n_gx :]
    block = pieces[0].shape[0]
    for k in range(n_gy):
        for j in range(n_gz):
            at = lax.rem(where[1] + n_gy - k, n_gy) * n_gz + lax.rem(where[2] + n_gz - j, n_gz)
            rows[pl.ds(pl.multiple_of(at * block, block), block), :] = pieces[k * n_gz + j][...]

    @pl.loop(0, weight.shape[1] // chunk)
    def _(c):
        span = pl.ds(pl.multiple_of(c * chunk, chunk), chunk)
        total[:, span] = jnp.dot(rows[...], weight[:, span], preferred_element_type=F32)

    part = outs[0].shape[0]
    for k in range(n_gx):
        at = pl.multiple_of(lax.rem(where[0] + k, n_gx) * part, part)
        outs[k][...] = total[pl.ds(at, part), :].astype(BF16)


def sum_split_body(n_gx, n_gy, n_gz, *refs):
    where = position()
    pieces, outs, total = refs[:n_gx], refs[n_gx : n_gx + n_gy], refs[-1]
    value = pieces[0][...].astype(F32)
    for piece in pieces[1:]:
        value = value + piece[...].astype(F32)
    each = outs[0].shape[1]
    for at in range(n_gy * n_gz):
        total[at] = value[at * each : (at + 1) * each]
    for k in range(n_gy):
        for j in range(n_gz):
            outs[k][j] = total[lax.rem(where[1] + k, n_gy) * n_gz + j].astype(BF16)


def attend_body(n_gy, n_gz, *refs):
    where = position()
    lengths, pieces, rest = refs[:n_gz], refs[n_gz : n_gz + n_gy], refs[n_gz + n_gy :]
    keys, values = rest[:n_gz], rest[n_gz : 2 * n_gz]
    outs, held, given = rest[2 * n_gz : -2], rest[-2], rest[-1]
    each, width = pieces[0].shape[1:]
    heads = width // HDIM
    lines = n_gy * heads
    half = held.shape[-1]
    halves = range(HDIM // half)
    sources = [lax.rem(where[2] + n_gz - j, n_gz) for j in range(n_gz)]
    for j in range(n_gz):
        for k in range(n_gy):
            mine = pieces[k][sources[j]].astype(F32)
            for h in range(heads):
                line = (k * heads + h) * each
                for p in halves:
                    at = h * HDIM + p * half
                    held[j, p, line : line + each, :] = mine[:, at : at + half]
    rows = [(j, r) for j in range(n_gz) for r in range(each)]
    scores = []
    for j, r in rows:
        span = pl.ds(r, lines, stride=each)
        query = jnp.concatenate([held[j, p, span, :] for p in halves], axis=1).astype(BF16)
        score = lax.dot_general(query, keys[j][r], (((1,), (1,)), ((), ())), preferred_element_type=F32)
        place = lax.broadcasted_iota(jnp.int32, score.shape, 1)
        scores.append(jnp.where(place < lengths[j][r], score * HDIM ** (-0.5), -jnp.inf))
    raised = [jnp.exp(score - jnp.max(score, axis=1, keepdims=True)) for score in scores]
    totals = [jnp.sum(weight, axis=1, keepdims=True) for weight in raised]
    for (j, r), weight, total in zip(rows, raised, totals):
        mixed = jnp.dot(weight.astype(BF16), values[j][r], preferred_element_type=F32) / total
        for p in halves:
            given[j, p, pl.ds(r, lines, stride=each), :] = mixed[:, p * half : (p + 1) * half]
    for j in range(n_gz):
        for k in range(n_gy):
            for h in range(heads):
                line = ((n_gy - k) % n_gy * heads + h) * each
                for p in halves:
                    at = h * HDIM + p * half
                    outs[k][sources[j], :, at : at + half] = given[j, p, line : line + each, :].astype(BF16)


def gather_rows_body(n_gy, n_gz, *refs):
    where = position()
    pieces, out, total = refs[:-2], refs[-2], refs[-1]
    for k in range(n_gy):
        for j in range(n_gz):
            total[lax.rem(where[1] + n_gy - k, n_gy) * n_gz + j] = pieces[k][j].astype(F32)
    out[...] = jnp.concatenate([total[i] for i in range(n_gy * n_gz)], axis=0).astype(BF16)


def output_body(n_gx, n_gy, n_gz, chunk, *refs):
    where = position()
    pieces, weight = refs[:n_gx], refs[n_gx]
    count = n_gy * n_gz
    outs = refs[n_gx + 1 : n_gx + 1 + count]
    rows, total = refs[n_gx + 1 + count :]
    block = pieces[0].shape[0]
    for k in range(n_gx):
        at = pl.multiple_of(lax.rem(where[0] + n_gx - k, n_gx) * block, block)
        rows[pl.ds(at, block), :] = pieces[k][...]
    part = outs[0].shape[0]

    @pl.loop(0, weight.shape[1] // chunk)
    def _(c):
        span = pl.ds(pl.multiple_of(c * chunk, chunk), chunk)
        total[...] = jnp.dot(rows[...], weight[:, span], preferred_element_type=F32)
        for k in range(n_gy):
            for j in range(n_gz):
                at = lax.rem(where[1] + k, n_gy) * n_gz + lax.rem(where[2] + j, n_gz)
                at = pl.multiple_of(at * part, part)
                outs[k * n_gz + j][:, span] = total[pl.ds(at, part), :].astype(BF16)


def sum_body(*refs):
    value = refs[0][...].astype(F32)
    for ref in refs[1:-1]:
        value = value + ref[...].astype(F32)
    refs[-1][...] = value.astype(BF16)


def added(arrays, name):
    out = jax.ShapeDtypeStruct(arrays[0].shape, BF16)
    return call(sum_body, [out], arrays, [VMEM] * len(arrays), name=name)[0]


def mib_for(*sizes):
    return max(8, -(-int(sum(sizes) * 1.25) // 2**20) + 2)


def shards(tokens, q_weight, o_weight, key_cache, value_cache, lengths):
    n_gx, n_gy, n_gz = (lax.axis_size(a) for a in ("gx", "gy", "gz"))
    own_rows, depth = tokens.shape
    row_count = own_rows * n_gy * n_gz
    width = q_weight.shape[1]
    each = key_cache.shape[0]
    part = row_count // n_gx
    struct = jax.ShapeDtypeStruct

    weight_bytes = 2 * depth * width
    staged = call(
        stage_body,
        [struct(tokens.shape, BF16)],
        [tokens],
        [ANY],
        scratch=[pltpu.SemaphoreType.DMA],
        beside=3000 * weight_bytes,
        name="own_tokens",
    )[0]
    pieces = []
    for k in range(n_gy):
        over = shift(tokens, "gy", k) if k else tokens
        pieces += [shift(over, "gz", j) if j else over for j in range(n_gz)]
    pieces[0] = staged
    chip_keys, chip_values, chip_lengths = (
        [array] + [shift(array, "gz", j) for j in range(1, n_gz)] for array in (key_cache, value_cache, lengths)
    )
    chunk = largest_divisor(width, 256, 128)
    terms = call(
        functools.partial(query_body, n_gx, n_gy, n_gz, chunk),
        [struct((part, width), BF16)] * n_gx,
        [*pieces, q_weight],
        [VMEM] * len(pieces) + [VMEM],
        scratch=[
            pltpu.VMEM((row_count, depth), BF16),
            pltpu.VMEM((row_count, width), F32),
        ],
        mib=mib_for(row_count * depth * 4, row_count * width * 8, depth * width * 2),
        flops=2 * row_count * depth * width,
        name="query_terms",
    )

    terms = [terms[0]] + [shift(terms[k], "gx", k) for k in range(1, n_gx)]
    queries = call(
        functools.partial(sum_split_body, n_gx, n_gy, n_gz),
        [struct((n_gz, each, width), BF16)] * n_gy,
        [*terms],
        [VMEM] * n_gx,
        scratch=[pltpu.VMEM((n_gy * n_gz, each, width), F32)],
        beside=20000 * key_cache.size,
        name="query_sum",
    )
    pieces = [shift(queries[k], "gy", k) if k else queries[k] for k in range(n_gy)]
    mixed = call(
        functools.partial(attend_body, n_gy, n_gz),
        [struct((n_gz, each, width), BF16)] * n_gy,
        [*chip_lengths, *pieces, *chip_keys, *chip_values],
        [SMEM] * n_gz + [VMEM] * (n_gy + 2 * n_gz),
        scratch=[pltpu.VMEM((n_gz, HDIM // 128, n_gy * width // HDIM * each, 128), F32)] * 2,
        mib=12,
        name="attention",
    )

    pieces = [shift(mixed[k], "gy", k) if k else mixed[k] for k in range(n_gy)]
    block = call(
        functools.partial(gather_rows_body, n_gy, n_gz),
        [struct((part, width), BF16)],
        pieces,
        [VMEM] * n_gy,
        scratch=[pltpu.VMEM((n_gy * n_gz, each, width), F32)],
        name="mixed_rows",
    )[0]
    blocks = [block] + [shift(block, "gx", k) for k in range(1, n_gx)]
    columns = o_weight.shape[1]
    chunk = largest_divisor(columns, 512, 128)
    terms = call(
        functools.partial(output_body, n_gx, n_gy, n_gz, chunk),
        [struct((own_rows, columns), BF16)] * (n_gy * n_gz),
        [*blocks, o_weight],
        [VMEM] * n_gx + [VMEM],
        scratch=[
            pltpu.VMEM((row_count, width), BF16),
            pltpu.VMEM((row_count, chunk), F32),
        ],
        mib=mib_for(row_count * width * 4, row_count * (chunk * 4 + columns * 2), columns * width * 2),
        flops=2 * row_count * columns * width,
        name="output_terms",
    )

    arrived = []
    for k in range(1, n_gy):
        mine = terms[k * n_gz : (k + 1) * n_gz]
        mine = [mine[0]] + [shift(mine[j], "gz", j) for j in range(1, n_gz)]
        arrived.append(shift(added(mine, "pair_sum") if n_gz > 1 else mine[0], "gy", k))
    mine = [terms[0]] + [shift(terms[j], "gz", j) for j in range(1, n_gz)]
    return added(mine + arrived, "output_sum")


def solution(mesh):
    return jax.shard_map(
        shards,
        mesh=mesh,
        in_specs=(
            P(("groups", "gy", "gz"), "gx"),
            P("gx", ("gy", "gz")),
            P(("gy", "gz"), "gx"),
            P(("groups", "gx", "gy", "gz"), None, None),
            P(("groups", "gx", "gy", "gz"), None, None),
            P(("groups", "gx", "gy", "gz")),
        ),
        out_specs=P(("groups", "gy", "gz"), "gx"),
        check_vma=False,
    )
```

```python
import functools

import jax
import jax.numpy as jnp
from jax import lax
from jax.experimental import pallas as pl
from jax.experimental.pallas import tpu as pltpu
from jax.sharding import PartitionSpec as P

HDIM = 256
BF16 = jnp.bfloat16
F32 = jnp.float32
VMEM = pl.BlockSpec(memory_space=pltpu.VMEM)
ANY = pl.BlockSpec(memory_space=pl.ANY)
SMEM = pl.BlockSpec(memory_space=pltpu.SMEM)


def shift(array, axis, by):
    size = lax.axis_size(axis)
    return lax.ppermute(array, axis, [(s, (s + by) % size) for s in range(size)])


def position():
    return tuple(lax.axis_index(a) for a in ("gx", "gy", "gz"))


def largest_divisor(extent, limit, unit):
    best = extent
    for size in range(unit, limit + 1, unit):
        if extent % size == 0:
            best = size
    return best


def call(body, outs, operands, in_specs, scratch=(), mib=8, flops=0, beside=0, name=None):
    moved = sum(a.size * a.dtype.itemsize for a in operands)
    moved += sum(o.size * o.dtype.itemsize for o in outs)
    return pl.pallas_call(
        body,
        out_shape=list(outs),
        in_specs=in_specs,
        out_specs=[VMEM] * len(outs),
        scratch_shapes=list(scratch),
        compiler_params=pltpu.CompilerParams(vmem_limit_bytes=mib * 2**20),
        cost_estimate=pl.CostEstimate(flops=flops + beside, bytes_accessed=moved, transcendentals=0),
        name=name,
    )(*operands)


def stage_body(tokens, out, sem):
    copy = pltpu.make_async_copy(tokens, out, sem)
    copy.start()
    copy.wait()


def product(rows, weight, span, step):
    total = None
    for at in range(0, weight.shape[0], step):
        deep = slice(at, min(at + step, weight.shape[0]))
        term = jnp.dot(rows[:, deep], weight[deep, span], preferred_element_type=F32)
        total = term if total is None else total + term
    return total


def clear_below(rows, count):
    if rows.shape[0] > count:
        rows[count:, :] = jnp.zeros((rows.shape[0] - count, rows.shape[1]), rows.dtype)


def query_body(n_gx, n_gy, n_gz, chunk, *refs):
    where = position()
    count = n_gy * n_gz
    pieces, weight = refs[:count], refs[count]
    outs = refs[count + 1 : count + 1 + n_gx]
    rows, total = refs[count + 1 + n_gx :]
    block = pieces[0].shape[0]
    for k in range(n_gy):
        for j in range(n_gz):
            at = lax.rem(where[1] + n_gy - k, n_gy) * n_gz + lax.rem(where[2] + n_gz - j, n_gz)
            rows[pl.ds(pl.multiple_of(at * block, block), block), :] = pieces[k * n_gz + j][...]
    count = block * n_gy * n_gz
    clear_below(rows, count)
    for c in range(weight.shape[1] // chunk):
        span = slice(c * chunk, (c + 1) * chunk)
        total[:, span] = product(rows, weight, span, 768)[:count]
    part = outs[0].shape[0]
    for k in range(n_gx):
        at = pl.multiple_of(lax.rem(where[0] + k, n_gx) * part, part)
        outs[k][...] = total[pl.ds(at, part), :].astype(BF16)


def sum_split_body(n_gx, n_gy, n_gz, *refs):
    where = position()
    pieces, outs, total = refs[:n_gx], refs[n_gx : n_gx + n_gy], refs[-1]
    value = pieces[0][...].astype(F32)
    for piece in pieces[1:]:
        value = value + piece[...].astype(F32)
    each = outs[0].shape[1]
    for at in range(n_gy * n_gz):
        total[at] = value[at * each : (at + 1) * each]
    for k in range(n_gy):
        for j in range(n_gz):
            outs[k][j] = total[lax.rem(where[1] + k, n_gy) * n_gz + j].astype(BF16)


def attend_body(n_gy, n_gz, *refs):
    where = position()
    lengths, pieces, rest = refs[:n_gz], refs[n_gz : n_gz + n_gy], refs[n_gz + n_gy :]
    keys, values = rest[:n_gz], rest[n_gz : 2 * n_gz]
    outs, held, given = rest[2 * n_gz : -2], rest[-2], rest[-1]
    each, width = pieces[0].shape[1:]
    heads = width // HDIM
    lines = n_gy * heads
    half = held.shape[-1]
    halves = range(HDIM // half)
    sources = [lax.rem(where[2] + n_gz - j, n_gz) for j in range(n_gz)]
    for j in range(n_gz):
        for k in range(n_gy):
            mine = pieces[k][sources[j]].astype(F32)
            for h in range(heads):
                line = (k * heads + h) * each
                for p in halves:
                    at = h * HDIM + p * half
                    held[j, p, line : line + each, :] = mine[:, at : at + half]
    rows = [(j, r) for j in range(n_gz) for r in range(each)]
    scores = []
    for j, r in rows:
        span = pl.ds(r, lines, stride=each)
        query = jnp.concatenate([held[j, p, span, :] for p in halves], axis=1).astype(BF16)
        score = lax.dot_general(query, keys[j][r], (((1,), (1,)), ((), ())), preferred_element_type=F32)
        place = lax.broadcasted_iota(jnp.int32, score.shape, 1)
        scores.append(jnp.where(place < lengths[j][r], score * HDIM ** (-0.5), -jnp.inf))
    raised = [jnp.exp(score - jnp.max(score, axis=1, keepdims=True)) for score in scores]
    totals = [jnp.sum(weight, axis=1, keepdims=True) for weight in raised]
    for (j, r), weight, total in zip(rows, raised, totals):
        mixed = jnp.dot(weight.astype(BF16), values[j][r], preferred_element_type=F32) / total
        for p in halves:
            given[j, p, pl.ds(r, lines, stride=each), :] = mixed[:, p * half : (p + 1) * half]
    for j in range(n_gz):
        for k in range(n_gy):
            for h in range(heads):
                line = ((n_gy - k) % n_gy * heads + h) * each
                for p in halves:
                    at = h * HDIM + p * half
                    outs[k][sources[j], :, at : at + half] = given[j, p, line : line + each, :].astype(BF16)


def gather_rows_body(n_gy, n_gz, *refs):
    where = position()
    pieces, out, total = refs[:-2], refs[-2], refs[-1]
    for k in range(n_gy):
        for j in range(n_gz):
            total[lax.rem(where[1] + n_gy - k, n_gy) * n_gz + j] = pieces[k][j].astype(F32)
    out[...] = jnp.concatenate([total[i] for i in range(n_gy * n_gz)], axis=0).astype(BF16)


def output_body(n_gx, n_gy, n_gz, chunk, *refs):
    where = position()
    pieces, weight = refs[:n_gx], refs[n_gx]
    count = n_gy * n_gz
    outs = refs[n_gx + 1 : n_gx + 1 + count]
    rows, total = refs[n_gx + 1 + count :]
    block = pieces[0].shape[0]
    for k in range(n_gx):
        at = pl.multiple_of(lax.rem(where[0] + n_gx - k, n_gx) * block, block)
        rows[pl.ds(at, block), :] = pieces[k][...]
    part = outs[0].shape[0]
    count = block * n_gx
    clear_below(rows, count)
    for c in range(weight.shape[1] // chunk):
        span = slice(c * chunk, (c + 1) * chunk)
        total[...] = product(rows, weight, span, 768)[:count]
        for k in range(n_gy):
            for j in range(n_gz):
                at = lax.rem(where[1] + k, n_gy) * n_gz + lax.rem(where[2] + j, n_gz)
                at = pl.multiple_of(at * part, part)
                outs[k * n_gz + j][:, span] = total[pl.ds(at, part), :].astype(BF16)


def sum_body(*refs):
    value = refs[0][...].astype(F32)
    for ref in refs[1:-1]:
        value = value + ref[...].astype(F32)
    refs[-1][...] = value.astype(BF16)


def added(arrays, name):
    out = jax.ShapeDtypeStruct(arrays[0].shape, BF16)
    return call(sum_body, [out], arrays, [VMEM] * len(arrays), name=name)[0]


def mib_for(*sizes):
    return max(8, -(-int(sum(sizes) * 1.25) // 2**20) + 2)


def shards(tokens, q_weight, o_weight, key_cache, value_cache, lengths):
    n_gx, n_gy, n_gz = (lax.axis_size(a) for a in ("gx", "gy", "gz"))
    own_rows, depth = tokens.shape
    row_count = own_rows * n_gy * n_gz
    width = q_weight.shape[1]
    each = key_cache.shape[0]
    tall = max(row_count, 128)
    part = row_count // n_gx
    struct = jax.ShapeDtypeStruct

    weight_bytes = 2 * depth * width
    staged = call(
        stage_body,
        [struct(tokens.shape, BF16)],
        [tokens],
        [ANY],
        scratch=[pltpu.SemaphoreType.DMA],
        beside=3000 * weight_bytes,
        name="own_tokens",
    )[0]
    pieces = []
    for k in range(n_gy):
        over = shift(tokens, "gy", k) if k else tokens
        pieces += [shift(over, "gz", j) if j else over for j in range(n_gz)]
    pieces[0] = staged
    chip_keys, chip_values, chip_lengths = (
        [array] + [shift(array, "gz", j) for j in range(1, n_gz)] for array in (key_cache, value_cache, lengths)
    )
    chunk = largest_divisor(width, 256, 128)
    terms = call(
        functools.partial(query_body, n_gx, n_gy, n_gz, chunk),
        [struct((part, width), BF16)] * n_gx,
        [*pieces, q_weight],
        [VMEM] * len(pieces) + [VMEM],
        scratch=[
            pltpu.VMEM((tall, depth), BF16),
            pltpu.VMEM((row_count, width), F32),
        ],
        mib=mib_for(tall * depth * 4, tall * width * 8, depth * width * 2),
        flops=2 * row_count * depth * width,
        name="query_terms",
    )

    terms = [terms[0]] + [shift(terms[k], "gx", k) for k in range(1, n_gx)]
    queries = call(
        functools.partial(sum_split_body, n_gx, n_gy, n_gz),
        [struct((n_gz, each, width), BF16)] * n_gy,
        [*terms],
        [VMEM] * n_gx,
        scratch=[pltpu.VMEM((n_gy * n_gz, each, width), F32)],
        beside=20000 * key_cache.size,
        name="query_sum",
    )
    pieces = [shift(queries[k], "gy", k) if k else queries[k] for k in range(n_gy)]
    mixed = call(
        functools.partial(attend_body, n_gy, n_gz),
        [struct((n_gz, each, width), BF16)] * n_gy,
        [*chip_lengths, *pieces, *chip_keys, *chip_values],
        [SMEM] * n_gz + [VMEM] * (n_gy + 2 * n_gz),
        scratch=[pltpu.VMEM((n_gz, HDIM // 128, n_gy * width // HDIM * each, 128), F32)] * 2,
        mib=12,
        name="attention",
    )

    pieces = [shift(mixed[k], "gy", k) if k else mixed[k] for k in range(n_gy)]
    block = call(
        functools.partial(gather_rows_body, n_gy, n_gz),
        [struct((part, width), BF16)],
        pieces,
        [VMEM] * n_gy,
        scratch=[pltpu.VMEM((n_gy * n_gz, each, width), F32)],
        name="mixed_rows",
    )[0]
    blocks = [block] + [shift(block, "gx", k) for k in range(1, n_gx)]
    columns = o_weight.shape[1]
    chunk = largest_divisor(columns, 768, 128)
    terms = call(
        functools.partial(output_body, n_gx, n_gy, n_gz, chunk),
        [struct((own_rows, columns), BF16)] * (n_gy * n_gz),
        [*blocks, o_weight],
        [VMEM] * n_gx + [VMEM],
        scratch=[
            pltpu.VMEM((tall, width), BF16),
            pltpu.VMEM((row_count, chunk), F32),
        ],
        mib=mib_for(tall * width * 4, tall * (chunk * 4 + columns * 2), columns * width * 2),
        flops=2 * row_count * columns * width,
        name="output_terms",
    )

    arrived = []
    for k in range(1, n_gy):
        mine = terms[k * n_gz : (k + 1) * n_gz]
        mine = [mine[0]] + [shift(mine[j], "gz", j) for j in range(1, n_gz)]
        arrived.append(shift(added(mine, "pair_sum") if n_gz > 1 else mine[0], "gy", k))
    mine = [terms[0]] + [shift(terms[j], "gz", j) for j in range(1, n_gz)]
    return added(mine + arrived, "output_sum")


def solution(mesh):
    return jax.shard_map(
        shards,
        mesh=mesh,
        in_specs=(
            P(("groups", "gy", "gz"), "gx"),
            P("gx", ("gy", "gz")),
            P(("gy", "gz"), "gx"),
            P(("groups", "gx", "gy", "gz"), None, None),
            P(("groups", "gx", "gy", "gz"), None, None),
            P(("groups", "gx", "gy", "gz")),
        ),
        out_specs=P(("groups", "gy", "gz"), "gx"),
        check_vma=False,
    )
```

```python
import functools

import jax
import jax.numpy as jnp
from jax import lax
from jax.experimental import pallas as pl
from jax.experimental.pallas import tpu as pltpu
from jax.sharding import PartitionSpec as P

HDIM = 256
BF16 = jnp.bfloat16
F32 = jnp.float32
VMEM = pl.BlockSpec(memory_space=pltpu.VMEM)
ANY = pl.BlockSpec(memory_space=pl.ANY)
SMEM = pl.BlockSpec(memory_space=pltpu.SMEM)


def shift(array, axis, by):
    size = lax.axis_size(axis)
    return lax.ppermute(array, axis, [(s, (s + by) % size) for s in range(size)])


def position():
    return tuple(lax.axis_index(a) for a in ("gx", "gy", "gz"))


def largest_divisor(extent, limit, unit):
    best = extent
    for size in range(unit, limit + 1, unit):
        if extent % size == 0:
            best = size
    return best


def call(body, outs, operands, in_specs, scratch=(), mib=8, flops=0, beside=0, name=None):
    moved = sum(a.size * a.dtype.itemsize for a in operands)
    moved += sum(o.size * o.dtype.itemsize for o in outs)
    return pl.pallas_call(
        body,
        out_shape=list(outs),
        in_specs=in_specs,
        out_specs=[VMEM] * len(outs),
        scratch_shapes=list(scratch),
        compiler_params=pltpu.CompilerParams(vmem_limit_bytes=mib * 2**20),
        cost_estimate=pl.CostEstimate(flops=flops + beside, bytes_accessed=moved, transcendentals=0),
        name=name,
    )(*operands)


def stage_body(tokens, out, sem):
    copy = pltpu.make_async_copy(tokens, out, sem)
    copy.start()
    copy.wait()


def product(rows, weight, span, step):
    total = None
    for at in range(0, weight.shape[0], step):
        deep = slice(at, min(at + step, weight.shape[0]))
        term = jnp.dot(rows[:, deep], weight[deep, span], preferred_element_type=F32)
        total = term if total is None else total + term
    return total


def clear_below(rows, count):
    if rows.shape[0] > count:
        rows[count:, :] = jnp.zeros((rows.shape[0] - count, rows.shape[1]), rows.dtype)


def query_body(n_gx, n_gy, n_gz, chunk, *refs):
    where = position()
    count = n_gy * n_gz
    pieces, weight = refs[:count], refs[count]
    outs = refs[count + 1 : count + 1 + n_gx]
    rows, total = refs[count + 1 + n_gx :]
    block = pieces[0].shape[0]
    for k in range(n_gy):
        for j in range(n_gz):
            at = lax.rem(where[1] + n_gy - k, n_gy) * n_gz + lax.rem(where[2] + n_gz - j, n_gz)
            rows[pl.ds(pl.multiple_of(at * block, block), block), :] = pieces[k * n_gz + j][...]
    count = block * n_gy * n_gz
    clear_below(rows, count)
    for c in range(weight.shape[1] // chunk):
        span = slice(c * chunk, (c + 1) * chunk)
        total[:, span] = product(rows, weight, span, 768)[:count]
    part = outs[0].shape[0]
    for k in range(n_gx):
        at = pl.multiple_of(lax.rem(where[0] + k, n_gx) * part, part)
        outs[k][...] = total[pl.ds(at, part), :].astype(BF16)


def sum_split_body(n_gx, n_gy, n_gz, *refs):
    where = position()
    pieces, outs, total = refs[:n_gx], refs[n_gx : n_gx + n_gy], refs[-1]
    value = pieces[0][...].astype(F32)
    for piece in pieces[1:]:
        value = value + piece[...].astype(F32)
    each = outs[0].shape[1]
    for at in range(n_gy * n_gz):
        total[at] = value[at * each : (at + 1) * each]
    for k in range(n_gy):
        for j in range(n_gz):
            outs[k][j] = total[lax.rem(where[1] + k, n_gy) * n_gz + j].astype(BF16)


def attend_body(n_gy, n_gz, *refs):
    where = position()
    lengths, pieces, rest = refs[:n_gz], refs[n_gz : n_gz + n_gy], refs[n_gz + n_gy :]
    keys, values = rest[:n_gz], rest[n_gz : 2 * n_gz]
    outs, held, given = rest[2 * n_gz : -2], rest[-2], rest[-1]
    each, width = pieces[0].shape[1:]
    heads = width // HDIM
    lines = n_gy * heads
    half = held.shape[-1]
    halves = range(HDIM // half)
    sources = [lax.rem(where[2] + n_gz - j, n_gz) for j in range(n_gz)]
    for j in range(n_gz):
        for k in range(n_gy):
            mine = pieces[k][sources[j]].astype(F32)
            for h in range(heads):
                line = (k * heads + h) * each
                for p in halves:
                    at = h * HDIM + p * half
                    held[j, p, line : line + each, :] = mine[:, at : at + half]
    rows = [(j, r) for j in range(n_gz) for r in range(each)]
    scores = []
    for j, r in rows:
        span = pl.ds(r, lines, stride=each)
        query = jnp.concatenate([held[j, p, span, :] for p in halves], axis=1).astype(BF16)
        score = lax.dot_general(query, keys[j][r], (((1,), (1,)), ((), ())), preferred_element_type=F32)
        place = lax.broadcasted_iota(jnp.int32, score.shape, 1)
        scores.append(jnp.where(place < lengths[j][r], score * HDIM ** (-0.5), -jnp.inf))
    raised = [jnp.exp(score - jnp.max(score, axis=1, keepdims=True)) for score in scores]
    totals = [jnp.sum(weight, axis=1, keepdims=True) for weight in raised]
    for (j, r), weight, total in zip(rows, raised, totals):
        mixed = jnp.dot(weight.astype(BF16), values[j][r], preferred_element_type=F32) / total
        for p in halves:
            given[j, p, pl.ds(r, lines, stride=each), :] = mixed[:, p * half : (p + 1) * half]
    for j in range(n_gz):
        for k in range(n_gy):
            for h in range(heads):
                line = ((n_gy - k) % n_gy * heads + h) * each
                for p in halves:
                    at = h * HDIM + p * half
                    outs[k][sources[j], :, at : at + half] = given[j, p, line : line + each, :].astype(BF16)


def gather_rows_body(n_gy, n_gz, *refs):
    where = position()
    pieces, outs, total = refs[:n_gy], refs[n_gy:-1], refs[-1]
    for k in range(n_gy):
        for j in range(n_gz):
            total[lax.rem(where[1] + n_gy - k, n_gy) * n_gz + j] = pieces[k][j].astype(F32)
    value = jnp.concatenate([total[i] for i in range(n_gy * n_gz)], axis=0).astype(BF16)
    for out in outs:
        out[...] = value


def output_body(n_gx, n_gy, n_gz, chunk, *refs):
    where = position()
    pieces, weight = refs[:n_gx], refs[n_gx]
    count = n_gy * n_gz
    outs = refs[n_gx + 1 : n_gx + 1 + count]
    rows, total = refs[n_gx + 1 + count :]
    block = pieces[0].shape[0]
    for k in range(n_gx):
        at = pl.multiple_of(lax.rem(where[0] + n_gx - k, n_gx) * block, block)
        rows[pl.ds(at, block), :] = pieces[k][...]
    part = outs[0].shape[0]
    count = block * n_gx
    clear_below(rows, count)
    for c in range(weight.shape[1] // chunk):
        span = slice(c * chunk, (c + 1) * chunk)
        total[...] = product(rows, weight, span, 768)[:count]
        for k in range(n_gy):
            for j in range(n_gz):
                at = lax.rem(where[1] + k, n_gy) * n_gz + lax.rem(where[2] + j, n_gz)
                at = pl.multiple_of(at * part, part)
                outs[k * n_gz + j][:, span] = total[pl.ds(at, part), :].astype(BF16)


def sum_body(*refs):
    value = refs[0][...].astype(F32)
    for ref in refs[1:-1]:
        value = value + ref[...].astype(F32)
    refs[-1][...] = value.astype(BF16)


def added(arrays, name):
    out = jax.ShapeDtypeStruct(arrays[0].shape, BF16)
    return call(sum_body, [out], arrays, [VMEM] * len(arrays), name=name)[0]


def mib_for(*sizes):
    return max(8, -(-int(sum(sizes) * 1.25) // 2**20) + 2)


def shards(tokens, q_weight, o_weight, key_cache, value_cache, lengths):
    n_gx, n_gy, n_gz = (lax.axis_size(a) for a in ("gx", "gy", "gz"))
    own_rows, depth = tokens.shape
    row_count = own_rows * n_gy * n_gz
    width = q_weight.shape[1]
    each = key_cache.shape[0]
    tall = max(row_count, 128)
    part = row_count // n_gx
    struct = jax.ShapeDtypeStruct

    weight_bytes = 2 * depth * width
    staged = call(
        stage_body,
        [struct(tokens.shape, BF16)],
        [tokens],
        [ANY],
        scratch=[pltpu.SemaphoreType.DMA],
        beside=3000 * weight_bytes,
        name="own_tokens",
    )[0]
    pieces = []
    for k in range(n_gy):
        over = shift(tokens, "gy", k) if k else tokens
        pieces += [shift(over, "gz", j) if j else over for j in range(n_gz)]
    pieces[0] = staged
    chip_keys, chip_values, chip_lengths = (
        [array] + [shift(array, "gz", j) for j in range(1, n_gz)] for array in (key_cache, value_cache, lengths)
    )
    chunk = largest_divisor(width, 256, 128)
    terms = call(
        functools.partial(query_body, n_gx, n_gy, n_gz, chunk),
        [struct((part, width), BF16)] * n_gx,
        [*pieces, q_weight],
        [VMEM] * len(pieces) + [VMEM],
        scratch=[
            pltpu.VMEM((tall, depth), BF16),
            pltpu.VMEM((row_count, width), F32),
        ],
        mib=mib_for(tall * depth * 4, tall * width * 8, depth * width * 2),
        flops=2 * row_count * depth * width,
        name="query_terms",
    )

    terms = [terms[0]] + [shift(terms[k], "gx", k) for k in range(1, n_gx)]
    queries = call(
        functools.partial(sum_split_body, n_gx, n_gy, n_gz),
        [struct((n_gz, each, width), BF16)] * n_gy,
        [*terms],
        [VMEM] * n_gx,
        scratch=[pltpu.VMEM((n_gy * n_gz, each, width), F32)],
        beside=20000 * key_cache.size,
        name="query_sum",
    )
    pieces = [shift(queries[k], "gy", k) if k else queries[k] for k in range(n_gy)]
    mixed = call(
        functools.partial(attend_body, n_gy, n_gz),
        [struct((n_gz, each, width), BF16)] * n_gy,
        [*chip_lengths, *pieces, *chip_keys, *chip_values],
        [SMEM] * n_gz + [VMEM] * (n_gy + 2 * n_gz),
        scratch=[pltpu.VMEM((n_gz, HDIM // 128, n_gy * width // HDIM * each, 128), F32)] * 2,
        mib=12,
        name="attention",
    )

    pieces = [shift(mixed[k], "gy", k) if k else mixed[k] for k in range(n_gy)]
    copies = call(
        functools.partial(gather_rows_body, n_gy, n_gz),
        [struct((part, width), BF16)] * n_gx,
        pieces,
        [VMEM] * n_gy,
        scratch=[pltpu.VMEM((n_gy * n_gz, each, width), F32)],
        name="mixed_rows",
    )
    blocks = [copies[0]] + [shift(copies[k], "gx", k) for k in range(1, n_gx)]
    columns = o_weight.shape[1]
    chunk = largest_divisor(columns, 768, 128)
    terms = call(
        functools.partial(output_body, n_gx, n_gy, n_gz, chunk),
        [struct((own_rows, columns), BF16)] * (n_gy * n_gz),
        [*blocks, o_weight],
        [VMEM] * n_gx + [VMEM],
        scratch=[
            pltpu.VMEM((tall, width), BF16),
            pltpu.VMEM((row_count, chunk), F32),
        ],
        mib=mib_for(tall * width * 4, tall * (chunk * 4 + columns * 2), columns * width * 2),
        flops=2 * row_count * columns * width,
        name="output_terms",
    )

    arrived = []
    for k in range(1, n_gy):
        mine = terms[k * n_gz : (k + 1) * n_gz]
        mine = [mine[0]] + [shift(mine[j], "gz", j) for j in range(1, n_gz)]
        arrived.append(shift(added(mine, "pair_sum") if n_gz > 1 else mine[0], "gy", k))
    mine = [terms[0]] + [shift(terms[j], "gz", j) for j in range(1, n_gz)]
    return added(mine + arrived, "output_sum")


def solution(mesh):
    return jax.shard_map(
        shards,
        mesh=mesh,
        in_specs=(
            P(("groups", "gy", "gz"), "gx"),
            P("gx", ("gy", "gz")),
            P(("gy", "gz"), "gx"),
            P(("groups", "gx", "gy", "gz"), None, None),
            P(("groups", "gx", "gy", "gz"), None, None),
            P(("groups", "gx", "gy", "gz")),
        ),
        out_specs=P(("groups", "gy", "gz"), "gx"),
        check_vma=False,
    )
```

```python
import functools

import jax
import jax.numpy as jnp
from jax import lax
from jax.experimental import pallas as pl
from jax.experimental.pallas import tpu as pltpu
from jax.sharding import PartitionSpec as P

HDIM = 256
BF16 = jnp.bfloat16
F32 = jnp.float32
VMEM = pl.BlockSpec(memory_space=pltpu.VMEM)
ANY = pl.BlockSpec(memory_space=pl.ANY)
SMEM = pl.BlockSpec(memory_space=pltpu.SMEM)


def shift(array, axis, by):
    size = lax.axis_size(axis)
    return lax.ppermute(array, axis, [(s, (s + by) % size) for s in range(size)])


def across():
    return 1 if lax.axis_size("gz") == 2 else 0


def hop(array, axis, by):
    size, cores = lax.axis_size(axis), lax.axis_size("gz")
    pairs = [
        (s * cores + c, (s + by) % size * cores + (c + across()) % cores) for s in range(size) for c in range(cores)
    ]
    return lax.ppermute(array, (axis, "gz"), pairs)


def hops(arrays, axis):
    return [hop(array, axis, by) if by else array for by, array in enumerate(arrays)]


def position():
    return tuple(lax.axis_index(a) for a in ("gx", "gy", "gz"))


def largest_divisor(extent, limit, unit):
    best = extent
    for size in range(unit, limit + 1, unit):
        if extent % size == 0:
            best = size
    return best


def call(body, outs, operands, in_specs, scratch=(), mib=8, flops=0, beside=0, name=None):
    moved = sum(a.size * a.dtype.itemsize for a in operands)
    moved += sum(o.size * o.dtype.itemsize for o in outs)
    return pl.pallas_call(
        body,
        out_shape=list(outs),
        in_specs=in_specs,
        out_specs=[VMEM] * len(outs),
        scratch_shapes=list(scratch),
        compiler_params=pltpu.CompilerParams(vmem_limit_bytes=mib * 2**20),
        cost_estimate=pl.CostEstimate(flops=flops + beside, bytes_accessed=moved, transcendentals=0),
        name=name,
    )(*operands)


def stage_body(tokens, out, sem):
    copy = pltpu.make_async_copy(tokens, out, sem)
    copy.start()
    copy.wait()


def product(rows, weight, span, step):
    total = None
    for at in range(0, weight.shape[0], step):
        deep = slice(at, min(at + step, weight.shape[0]))
        term = jnp.dot(rows[:, deep], weight[deep, span], preferred_element_type=F32)
        total = term if total is None else total + term
    return total


def clear_below(rows, count):
    if rows.shape[0] > count:
        rows[count:, :] = jnp.zeros((rows.shape[0] - count, rows.shape[1]), rows.dtype)


def query_body(n_gx, n_gy, n_gz, chunk, *refs):
    where = position()
    count = n_gy * n_gz
    pieces, weight = refs[:count], refs[count]
    outs = refs[count + 1 : count + 1 + n_gx]
    rows, total = refs[count + 1 + n_gx :]
    block = pieces[0].shape[0]
    for k in range(n_gy):
        for j in range(n_gz):
            core = where[2] + n_gz - j
            at = lax.rem(where[1] + n_gy - k, n_gy) * n_gz + lax.rem(core, n_gz)
            rows[pl.ds(pl.multiple_of(at * block, block), block), :] = pieces[k * n_gz + j][...]
    count = block * n_gy * n_gz
    clear_below(rows, count)
    for c in range(weight.shape[1] // chunk):
        span = slice(c * chunk, (c + 1) * chunk)
        total[:, span] = product(rows, weight, span, 768)[:count]
    part = outs[0].shape[0]
    for k in range(n_gx):
        at = pl.multiple_of(lax.rem(where[0] + k, n_gx) * part, part)
        outs[k][...] = total[pl.ds(at, part), :].astype(BF16)


def sum_split_body(n_gx, n_gy, n_gz, *refs):
    where = position()
    pieces, outs, total = refs[:n_gx], refs[n_gx : n_gx + n_gy], refs[-1]
    value = pieces[0][...].astype(F32)
    for piece in pieces[1:]:
        value = value + piece[...].astype(F32)
    each = outs[0].shape[1]
    for at in range(n_gy * n_gz):
        total[at] = value[at * each : (at + 1) * each]
    for k in range(n_gy):
        for j in range(n_gz):
            outs[k][j] = total[lax.rem(where[1] + k, n_gy) * n_gz + j].astype(BF16)


def attend_body(n_gy, n_gz, *refs):
    where = position()
    lengths, pieces, rest = refs[:n_gz], refs[n_gz : n_gz + n_gy], refs[n_gz + n_gy :]
    keys, values = rest[:n_gz], rest[n_gz : 2 * n_gz]
    outs, held, given = rest[2 * n_gz : -2], rest[-2], rest[-1]
    each, width = pieces[0].shape[1:]
    heads = width // HDIM
    lines = n_gy * heads
    half = held.shape[-1]
    halves = range(HDIM // half)
    sources = [lax.rem(where[2] + n_gz - j, n_gz) for j in range(n_gz)]
    for j in range(n_gz):
        for k in range(n_gy):
            mine = pieces[k][sources[j]].astype(F32)
            for h in range(heads):
                line = (k * heads + h) * each
                for p in halves:
                    at = h * HDIM + p * half
                    held[j, p, line : line + each, :] = mine[:, at : at + half]
    rows = [(j, r) for j in range(n_gz) for r in range(each)]
    scores = []
    for j, r in rows:
        span = pl.ds(r, lines, stride=each)
        query = jnp.concatenate([held[j, p, span, :] for p in halves], axis=1).astype(BF16)
        score = lax.dot_general(query, keys[j][r], (((1,), (1,)), ((), ())), preferred_element_type=F32)
        place = lax.broadcasted_iota(jnp.int32, score.shape, 1)
        scores.append(jnp.where(place < lengths[j][r], score * HDIM ** (-0.5), -jnp.inf))
    raised = [jnp.exp(score - jnp.max(score, axis=1, keepdims=True)) for score in scores]
    totals = [jnp.sum(weight, axis=1, keepdims=True) for weight in raised]
    for (j, r), weight, total in zip(rows, raised, totals):
        mixed = jnp.dot(weight.astype(BF16), values[j][r], preferred_element_type=F32) / total
        for p in halves:
            given[j, p, pl.ds(r, lines, stride=each), :] = mixed[:, p * half : (p + 1) * half]
    for j in range(n_gz):
        for k in range(n_gy):
            for h in range(heads):
                line = ((n_gy - k) % n_gy * heads + h) * each
                for p in halves:
                    at = h * HDIM + p * half
                    outs[k][sources[j], :, at : at + half] = given[j, p, line : line + each, :].astype(BF16)


def gather_rows_body(n_gy, n_gz, *refs):
    where = position()
    pieces, outs, total = refs[:n_gy], refs[n_gy:-1], refs[-1]
    for k in range(n_gy):
        for j in range(n_gz):
            total[lax.rem(where[1] + n_gy - k, n_gy) * n_gz + j] = pieces[k][j].astype(F32)
    value = jnp.concatenate([total[i] for i in range(n_gy * n_gz)], axis=0).astype(BF16)
    for out in outs:
        out[...] = value


def output_body(n_gx, n_gy, n_gz, chunk, *refs):
    where = position()
    pieces, weight = refs[:n_gx], refs[n_gx]
    count = n_gy * n_gz
    outs = refs[n_gx + 1 : n_gx + 1 + count]
    rows, total = refs[n_gx + 1 + count :]
    block = pieces[0].shape[0]
    for k in range(n_gx):
        at = pl.multiple_of(lax.rem(where[0] + n_gx - k, n_gx) * block, block)
        rows[pl.ds(at, block), :] = pieces[k][...]
    part = outs[0].shape[0]
    count = block * n_gx
    clear_below(rows, count)
    for c in range(weight.shape[1] // chunk):
        span = slice(c * chunk, (c + 1) * chunk)
        total[...] = product(rows, weight, span, 768)[:count]
        for k in range(n_gy):
            for j in range(n_gz):
                at = lax.rem(where[1] + k, n_gy) * n_gz + lax.rem(where[2] + j, n_gz)
                at = pl.multiple_of(at * part, part)
                outs[k * n_gz + j][:, span] = total[pl.ds(at, part), :].astype(BF16)


def sum_body(*refs):
    value = refs[0][...].astype(F32)
    for ref in refs[1:-1]:
        value = value + ref[...].astype(F32)
    refs[-1][...] = value.astype(BF16)


def added(arrays, name):
    out = jax.ShapeDtypeStruct(arrays[0].shape, BF16)
    return call(sum_body, [out], arrays, [VMEM] * len(arrays), name=name)[0]


def mib_for(*sizes):
    return max(8, -(-int(sum(sizes) * 1.25) // 2**20) + 2)


def shards(tokens, q_weight, o_weight, key_cache, value_cache, lengths):
    n_gx, n_gy, n_gz = (lax.axis_size(a) for a in ("gx", "gy", "gz"))
    own_rows, depth = tokens.shape
    row_count = own_rows * n_gy * n_gz
    width = q_weight.shape[1]
    each = key_cache.shape[0]
    tall = max(row_count, 128)
    part = row_count // n_gx
    struct = jax.ShapeDtypeStruct

    weight_bytes = 2 * depth * width
    staged = call(
        stage_body,
        [struct(tokens.shape, BF16)],
        [tokens],
        [ANY],
        scratch=[pltpu.SemaphoreType.DMA],
        beside=3000 * weight_bytes,
        name="own_tokens",
    )[0]
    pieces = []
    for k in range(n_gy):
        over = shift(tokens, "gy", k) if k else tokens
        pieces += [shift(over, "gz", j) if j else over for j in range(n_gz)]
    pieces[0] = staged
    chip_keys, chip_values, chip_lengths = (
        [array] + [shift(array, "gz", j) for j in range(1, n_gz)] for array in (key_cache, value_cache, lengths)
    )
    chunk = largest_divisor(width, 256, 128)
    terms = call(
        functools.partial(query_body, n_gx, n_gy, n_gz, chunk),
        [struct((part, width), BF16)] * n_gx,
        [*pieces, q_weight],
        [VMEM] * len(pieces) + [VMEM],
        scratch=[
            pltpu.VMEM((tall, depth), BF16),
            pltpu.VMEM((row_count, width), F32),
        ],
        mib=mib_for(tall * depth * 4, tall * width * 8, depth * width * 2),
        flops=2 * row_count * depth * width,
        name="query_terms",
    )

    terms = [terms[0]] + [shift(terms[k], "gx", k) for k in range(1, n_gx)]
    queries = call(
        functools.partial(sum_split_body, n_gx, n_gy, n_gz),
        [struct((n_gz, each, width), BF16)] * n_gy,
        [*terms],
        [VMEM] * n_gx,
        scratch=[pltpu.VMEM((n_gy * n_gz, each, width), F32)],
        beside=20000 * key_cache.size,
        name="query_sum",
    )
    pieces = hops(queries, "gy")
    mixed = call(
        functools.partial(attend_body, n_gy, n_gz),
        [struct((n_gz, each, width), BF16)] * n_gy,
        [*chip_lengths, *pieces, *chip_keys, *chip_values],
        [SMEM] * n_gz + [VMEM] * (n_gy + 2 * n_gz),
        scratch=[pltpu.VMEM((n_gz, HDIM // 128, n_gy * width // HDIM * each, 128), F32)] * 2,
        mib=12,
        name="attention",
    )

    pieces = hops(mixed, "gy")
    copies = call(
        functools.partial(gather_rows_body, n_gy, n_gz),
        [struct((part, width), BF16)] * n_gx,
        pieces,
        [VMEM] * n_gy,
        scratch=[pltpu.VMEM((n_gy * n_gz, each, width), F32)],
        name="mixed_rows",
    )
    blocks = [copies[0]] + [shift(copies[k], "gx", k) for k in range(1, n_gx)]
    columns = o_weight.shape[1]
    chunk = largest_divisor(columns, 768, 128)
    terms = call(
        functools.partial(output_body, n_gx, n_gy, n_gz, chunk),
        [struct((own_rows, columns), BF16)] * (n_gy * n_gz),
        [*blocks, o_weight],
        [VMEM] * n_gx + [VMEM],
        scratch=[
            pltpu.VMEM((tall, width), BF16),
            pltpu.VMEM((row_count, chunk), F32),
        ],
        mib=mib_for(tall * width * 4, tall * (chunk * 4 + columns * 2), columns * width * 2),
        flops=2 * row_count * columns * width,
        name="output_terms",
    )

    arrived = []
    for k in range(1, n_gy):
        mine = [terms[k * n_gz + j] for j in range(n_gz)]
        mine = [mine[0]] + [shift(mine[j], "gz", j) for j in range(1, n_gz)]
        arrived.append(shift(added(mine, "pair_sum") if n_gz > 1 else mine[0], "gy", k))
    mine = [terms[0]] + [shift(terms[j], "gz", j) for j in range(1, n_gz)]
    return added(mine + arrived, "output_sum")


def solution(mesh):
    return jax.shard_map(
        shards,
        mesh=mesh,
        in_specs=(
            P(("groups", "gy", "gz"), "gx"),
            P("gx", ("gy", "gz")),
            P(("gy", "gz"), "gx"),
            P(("groups", "gx", "gy", "gz"), None, None),
            P(("groups", "gx", "gy", "gz"), None, None),
            P(("groups", "gx", "gy", "gz")),
        ),
        out_specs=P(("groups", "gy", "gz"), "gx"),
        check_vma=False,
    )
```

```python
import functools

import jax
import jax.numpy as jnp
from jax import lax
from jax.experimental import pallas as pl
from jax.experimental.pallas import tpu as pltpu
from jax.sharding import PartitionSpec as P

HDIM = 256
BF16 = jnp.bfloat16
F32 = jnp.float32
VMEM = pl.BlockSpec(memory_space=pltpu.VMEM)
ANY = pl.BlockSpec(memory_space=pl.ANY)
SMEM = pl.BlockSpec(memory_space=pltpu.SMEM)


def shift(array, axis, by):
    size = lax.axis_size(axis)
    return lax.ppermute(array, axis, [(s, (s + by) % size) for s in range(size)])


def across():
    return 1 if lax.axis_size("gz") == 2 else 0


def hop(array, axis, by):
    size, cores = lax.axis_size(axis), lax.axis_size("gz")
    pairs = [
        (s * cores + c, (s + by) % size * cores + (c + across()) % cores) for s in range(size) for c in range(cores)
    ]
    return lax.ppermute(array, (axis, "gz"), pairs)


def hops(arrays, axis):
    return [hop(array, axis, by) if by else array for by, array in enumerate(arrays)]


def position():
    return tuple(lax.axis_index(a) for a in ("gx", "gy", "gz"))


def largest_divisor(extent, limit, unit):
    best = extent
    for size in range(unit, limit + 1, unit):
        if extent % size == 0:
            best = size
    return best


def call(body, outs, operands, in_specs, scratch=(), mib=8, flops=0, beside=0, name=None):
    moved = sum(a.size * a.dtype.itemsize for a in operands)
    moved += sum(o.size * o.dtype.itemsize for o in outs)
    return pl.pallas_call(
        body,
        out_shape=list(outs),
        in_specs=in_specs,
        out_specs=[VMEM] * len(outs),
        scratch_shapes=list(scratch),
        compiler_params=pltpu.CompilerParams(vmem_limit_bytes=mib * 2**20),
        cost_estimate=pl.CostEstimate(flops=flops + beside, bytes_accessed=moved, transcendentals=0),
        name=name,
    )(*operands)


def stage_body(tokens, out, sem):
    copy = pltpu.make_async_copy(tokens, out, sem)
    copy.start()
    copy.wait()


def product(rows, weight, span, step):
    total = None
    for at in range(0, weight.shape[0], step):
        deep = slice(at, min(at + step, weight.shape[0]))
        term = jnp.dot(rows[:, deep], weight[deep, span], preferred_element_type=F32)
        total = term if total is None else total + term
    return total


def clear_below(rows, count):
    if rows.shape[0] > count:
        rows[count:, :] = jnp.zeros((rows.shape[0] - count, rows.shape[1]), rows.dtype)


def query_body(n_gx, n_gy, n_gz, chunk, *refs):
    where = position()
    count = n_gy * n_gz
    pieces, weight = refs[:count], refs[count]
    outs = refs[count + 1 : count + 1 + n_gx]
    rows, total = refs[count + 1 + n_gx :]
    block = pieces[0].shape[0]
    for k in range(n_gy):
        for j in range(n_gz):
            core = where[2] + n_gz - j
            at = lax.rem(where[1] + n_gy - k, n_gy) * n_gz + lax.rem(core, n_gz)
            rows[pl.ds(pl.multiple_of(at * block, block), block), :] = pieces[k * n_gz + j][...]
    count = block * n_gy * n_gz
    clear_below(rows, count)
    for c in range(weight.shape[1] // chunk):
        span = slice(c * chunk, (c + 1) * chunk)
        total[:, span] = product(rows, weight, span, 768)[:count]
    part = outs[0].shape[0]
    for k in range(n_gx):
        at = pl.multiple_of(lax.rem(where[0] + k, n_gx) * part, part)
        outs[k][...] = total[pl.ds(at, part), :].astype(BF16)


def sum_split_body(n_gx, n_gy, n_gz, *refs):
    where = position()
    pieces, outs, total = refs[:n_gx], refs[n_gx : n_gx + n_gy], refs[-1]
    value = pieces[0][...].astype(F32)
    for piece in pieces[1:]:
        value = value + piece[...].astype(F32)
    each = outs[0].shape[1]
    for at in range(n_gy * n_gz):
        total[at] = value[at * each : (at + 1) * each]
    for k in range(n_gy):
        for j in range(n_gz):
            outs[k][j] = total[lax.rem(where[1] + k, n_gy) * n_gz + j].astype(BF16)


def attend_body(n_gy, n_gz, *refs):
    where = position()
    lengths, pieces, rest = refs[:n_gz], refs[n_gz : n_gz + n_gy], refs[n_gz + n_gy :]
    keys, values = rest[:n_gz], rest[n_gz : 2 * n_gz]
    outs, held, given = rest[2 * n_gz : -2], rest[-2], rest[-1]
    each, width = pieces[0].shape[1:]
    heads = width // HDIM
    lines = n_gy * heads
    half = held.shape[-1]
    halves = range(HDIM // half)
    sources = [lax.rem(where[2] + n_gz - j, n_gz) for j in range(n_gz)]
    for j in range(n_gz):
        for k in range(n_gy):
            mine = pieces[k][sources[j]].astype(F32)
            for h in range(heads):
                line = (k * heads + h) * each
                for p in halves:
                    at = h * HDIM + p * half
                    held[j, p, line : line + each, :] = mine[:, at : at + half]
    rows = [(j, r) for j in range(n_gz) for r in range(each)]
    scores = []
    for j, r in rows:
        span = pl.ds(r, lines, stride=each)
        query = jnp.concatenate([held[j, p, span, :] for p in halves], axis=1).astype(BF16)
        score = lax.dot_general(query, keys[j][r], (((1,), (1,)), ((), ())), preferred_element_type=F32)
        place = lax.broadcasted_iota(jnp.int32, score.shape, 1)
        scores.append(jnp.where(place < lengths[j][r], score * HDIM ** (-0.5), -jnp.inf))
    raised = [jnp.exp(score - jnp.max(score, axis=1, keepdims=True)) for score in scores]
    totals = [jnp.sum(weight, axis=1, keepdims=True) for weight in raised]
    for (j, r), weight, total in zip(rows, raised, totals):
        mixed = jnp.dot(weight.astype(BF16), values[j][r], preferred_element_type=F32) / total
        for p in halves:
            given[j, p, pl.ds(r, lines, stride=each), :] = mixed[:, p * half : (p + 1) * half]
    for j in range(n_gz):
        for k in range(n_gy):
            for h in range(heads):
                line = ((n_gy - k) % n_gy * heads + h) * each
                for p in halves:
                    at = h * HDIM + p * half
                    outs[k][sources[j], :, at : at + half] = given[j, p, line : line + each, :].astype(BF16)


def gather_rows_body(n_gy, n_gz, *refs):
    where = position()
    pieces, outs, total = refs[:n_gy], refs[n_gy:-1], refs[-1]
    for k in range(n_gy):
        for j in range(n_gz):
            total[lax.rem(where[1] + n_gy - k, n_gy) * n_gz + j] = pieces[k][j].astype(F32)
    value = jnp.concatenate([total[i] for i in range(n_gy * n_gz)], axis=0).astype(BF16)
    for out in outs:
        out[...] = value


def output_body(n_gx, n_gy, n_gz, chunk, first, *refs):
    where = position()
    pieces, weight = refs[:n_gx], refs[n_gx]
    count = n_gy * n_gz
    outs = refs[n_gx + 1 : n_gx + 1 + count]
    rows, total = refs[n_gx + 1 + count :]
    block = pieces[0].shape[0]
    for k in range(n_gx):
        at = pl.multiple_of(lax.rem(where[0] + n_gx - k, n_gx) * block, block)
        rows[pl.ds(at, block), :] = pieces[k][...]
    part = outs[0].shape[0]
    count = block * n_gx
    clear_below(rows, count)
    for c in range(outs[0].shape[1] // chunk):
        span = slice(first + c * chunk, first + (c + 1) * chunk)
        total[...] = product(rows, weight, span, 768)[:count]
        for k in range(n_gy):
            for j in range(n_gz):
                at = lax.rem(where[1] + k, n_gy) * n_gz + lax.rem(where[2] + j, n_gz)
                at = pl.multiple_of(at * part, part)
                outs[k * n_gz + j][:, c * chunk : (c + 1) * chunk] = total[pl.ds(at, part), :].astype(BF16)


def sum_body(*refs):
    value = refs[0][...].astype(F32)
    for ref in refs[1:-1]:
        value = value + ref[...].astype(F32)
    refs[-1][...] = value.astype(BF16)


def sum_parts_body(*refs):
    pieces, out = refs[:-1], refs[-1]
    wide = pieces[0].shape[1]
    each = len(pieces) // (out.shape[1] // wide)
    for c in range(out.shape[1] // wide):
        value = pieces[c * each][...].astype(F32)
        for piece in pieces[c * each + 1 : (c + 1) * each]:
            value = value + piece[...].astype(F32)
        out[:, c * wide : (c + 1) * wide] = value.astype(BF16)


def added(arrays, name):
    out = jax.ShapeDtypeStruct(arrays[0].shape, BF16)
    return call(sum_body, [out], arrays, [VMEM] * len(arrays), name=name)[0]


def mib_for(*sizes):
    return max(8, -(-int(sum(sizes) * 1.25) // 2**20) + 2)


def shards(tokens, q_weight, o_weight, key_cache, value_cache, lengths):
    n_gx, n_gy, n_gz = (lax.axis_size(a) for a in ("gx", "gy", "gz"))
    own_rows, depth = tokens.shape
    row_count = own_rows * n_gy * n_gz
    width = q_weight.shape[1]
    each = key_cache.shape[0]
    tall = max(row_count, 128)
    part = row_count // n_gx
    struct = jax.ShapeDtypeStruct

    weight_bytes = 2 * depth * width
    staged = call(
        stage_body,
        [struct(tokens.shape, BF16)],
        [tokens],
        [ANY],
        scratch=[pltpu.SemaphoreType.DMA],
        beside=3000 * weight_bytes,
        name="own_tokens",
    )[0]
    pieces = []
    for k in range(n_gy):
        over = shift(tokens, "gy", k) if k else tokens
        pieces += [shift(over, "gz", j) if j else over for j in range(n_gz)]
    pieces[0] = staged
    chip_keys, chip_values, chip_lengths = (
        [array] + [shift(array, "gz", j) for j in range(1, n_gz)] for array in (key_cache, value_cache, lengths)
    )
    pieces, chip_keys, chip_values, chip_lengths = lax.optimization_barrier(
        (pieces, chip_keys, chip_values, chip_lengths)
    )
    chunk = largest_divisor(width, 256, 128)
    terms = call(
        functools.partial(query_body, n_gx, n_gy, n_gz, chunk),
        [struct((part, width), BF16)] * n_gx,
        [*pieces, q_weight],
        [VMEM] * len(pieces) + [VMEM],
        scratch=[
            pltpu.VMEM((tall, depth), BF16),
            pltpu.VMEM((row_count, width), F32),
        ],
        mib=mib_for(tall * depth * 4, tall * width * 8, depth * width * 2),
        flops=2 * row_count * depth * width,
        name="query_terms",
    )

    terms = [terms[0]] + [shift(terms[k], "gx", k) for k in range(1, n_gx)]
    queries = call(
        functools.partial(sum_split_body, n_gx, n_gy, n_gz),
        [struct((n_gz, each, width), BF16)] * n_gy,
        [*terms],
        [VMEM] * n_gx,
        scratch=[pltpu.VMEM((n_gy * n_gz, each, width), F32)],
        beside=20000 * key_cache.size,
        name="query_sum",
    )
    pieces = hops(queries, "gy")
    mixed = call(
        functools.partial(attend_body, n_gy, n_gz),
        [struct((n_gz, each, width), BF16)] * n_gy,
        [*chip_lengths, *pieces, *chip_keys, *chip_values],
        [SMEM] * n_gz + [VMEM] * (n_gy + 2 * n_gz),
        scratch=[pltpu.VMEM((n_gz, HDIM // 128, n_gy * width // HDIM * each, 128), F32)] * 2,
        mib=12,
        name="attention",
    )

    pieces = hops(mixed, "gy")
    copies = call(
        functools.partial(gather_rows_body, n_gy, n_gz),
        [struct((part, width), BF16)] * n_gx,
        pieces,
        [VMEM] * n_gy,
        scratch=[pltpu.VMEM((n_gy * n_gz, each, width), F32)],
        name="mixed_rows",
    )
    blocks = [copies[0]] + [shift(copies[k], "gx", k) for k in range(1, n_gx)]
    columns = o_weight.shape[1]
    splits = 2 if columns % 512 == 0 else 1
    wide = columns // splits
    chunk = largest_divisor(wide, 768, 128)
    terms = [
        call(
            functools.partial(output_body, n_gx, n_gy, n_gz, chunk, c * wide),
            [struct((own_rows, wide), BF16)] * (n_gy * n_gz),
            [*blocks, o_weight],
            [VMEM] * (n_gx + 1),
            scratch=[pltpu.VMEM((tall, width), BF16), pltpu.VMEM((row_count, chunk), F32)],
            mib=mib_for(tall * width * 4, tall * (chunk * 4 + wide * 2), columns * width * 2),
            flops=2 * tall * wide * width,
            name="output_terms",
        )
        for c in range(splits)
    ]

    leaving, arrived = [], []
    for term in terms:
        for k in range(1, n_gy):
            mine = term[k * n_gz : (k + 1) * n_gz]
            mine = [mine[0]] + [shift(mine[j], "gz", j) for j in range(1, n_gz)]
            leaving.append(added(mine, "pair_sum") if n_gz > 1 else mine[0])
    for at, array in enumerate(leaving):
        arrived.append(shift(array, "gy", at % (n_gy - 1) + 1))
    staying = [term[j] for term in terms for j in range(1, n_gz)]
    if leaving and staying:
        leaving, staying = lax.optimization_barrier((leaving, staying))
    operands = []
    for c, term in enumerate(terms):
        operands.append(term[0])
        operands += [shift(staying[c * (n_gz - 1) + j - 1], "gz", j) for j in range(1, n_gz)]
        operands += arrived[c * (n_gy - 1) : (c + 1) * (n_gy - 1)]
    return call(
        sum_parts_body,
        [struct((own_rows, columns), BF16)],
        operands,
        [VMEM] * len(operands),
        name="output_sum",
    )[0]


def solution(mesh):
    return jax.shard_map(
        shards,
        mesh=mesh,
        in_specs=(
            P(("groups", "gy", "gz"), "gx"),
            P("gx", ("gy", "gz")),
            P(("gy", "gz"), "gx"),
            P(("groups", "gx", "gy", "gz"), None, None),
            P(("groups", "gx", "gy", "gz"), None, None),
            P(("groups", "gx", "gy", "gz")),
        ),
        out_specs=P(("groups", "gy", "gz"), "gx"),
        check_vma=False,
    )
```

```python
import functools

import jax
import jax.numpy as jnp
from jax import lax
from jax.experimental import pallas as pl
from jax.experimental.pallas import tpu as pltpu
from jax.sharding import PartitionSpec as P

HDIM = 256
BF16 = jnp.bfloat16
F32 = jnp.float32
VMEM = pl.BlockSpec(memory_space=pltpu.VMEM)
ANY = pl.BlockSpec(memory_space=pl.ANY)
SMEM = pl.BlockSpec(memory_space=pltpu.SMEM)


def shift(array, axis, by):
    size = lax.axis_size(axis)
    return lax.ppermute(array, axis, [(s, (s + by) % size) for s in range(size)])


def across():
    return 1 if lax.axis_size("gz") == 2 else 0


def hop(array, axis, by):
    size, cores = lax.axis_size(axis), lax.axis_size("gz")
    pairs = [
        (s * cores + c, (s + by) % size * cores + (c + across()) % cores) for s in range(size) for c in range(cores)
    ]
    return lax.ppermute(array, (axis, "gz"), pairs)


def hops(arrays, axis):
    return [hop(array, axis, by) if by else array for by, array in enumerate(arrays)]


def position():
    return tuple(lax.axis_index(a) for a in ("gx", "gy", "gz"))


def largest_divisor(extent, limit, unit):
    best = extent
    for size in range(unit, limit + 1, unit):
        if extent % size == 0:
            best = size
    return best


def call(body, outs, operands, in_specs, scratch=(), mib=8, flops=0, beside=0, name=None):
    moved = sum(a.size * a.dtype.itemsize for a in operands)
    moved += sum(o.size * o.dtype.itemsize for o in outs)
    return pl.pallas_call(
        body,
        out_shape=list(outs),
        in_specs=in_specs,
        out_specs=[VMEM] * len(outs),
        scratch_shapes=list(scratch),
        compiler_params=pltpu.CompilerParams(vmem_limit_bytes=mib * 2**20),
        cost_estimate=pl.CostEstimate(flops=flops + beside, bytes_accessed=moved, transcendentals=0),
        name=name,
    )(*operands)


def stage_body(tokens, out, sem):
    copy = pltpu.make_async_copy(tokens, out, sem)
    copy.start()
    copy.wait()


def product(rows, weight, span, step):
    total = None
    for at in range(0, weight.shape[0], step):
        deep = slice(at, min(at + step, weight.shape[0]))
        term = jnp.dot(rows[:, deep], weight[deep, span], preferred_element_type=F32)
        total = term if total is None else total + term
    return total


def clear_below(rows, count):
    if rows.shape[0] > count:
        rows[count:, :] = jnp.zeros((rows.shape[0] - count, rows.shape[1]), rows.dtype)


def query_body(n_gx, n_gy, n_gz, chunk, *refs):
    where = position()
    count = n_gy * n_gz
    pieces, weight = refs[:count], refs[count]
    outs = refs[count + 1 : count + 1 + n_gx]
    rows, total = refs[count + 1 + n_gx :]
    block = pieces[0].shape[0]
    for k in range(n_gy):
        for j in range(n_gz):
            core = where[2] + n_gz - j
            at = lax.rem(where[1] + n_gy - k, n_gy) * n_gz + lax.rem(core, n_gz)
            rows[pl.ds(pl.multiple_of(at * block, block), block), :] = pieces[k * n_gz + j][...]
    count = block * n_gy * n_gz
    clear_below(rows, count)
    for c in range(weight.shape[1] // chunk):
        span = slice(c * chunk, (c + 1) * chunk)
        total[:, span] = product(rows, weight, span, 768)[:count]
    part = outs[0].shape[0]
    for k in range(n_gx):
        at = pl.multiple_of(lax.rem(where[0] + k, n_gx) * part, part)
        outs[k][...] = total[pl.ds(at, part), :].astype(BF16)


def sum_split_body(n_gx, n_gy, n_gz, *refs):
    where = position()
    pieces, outs, total = refs[:n_gx], refs[n_gx : n_gx + n_gy], refs[-1]
    value = pieces[0][...].astype(F32)
    for piece in pieces[1:]:
        value = value + piece[...].astype(F32)
    each = outs[0].shape[1]
    for at in range(n_gy * n_gz):
        total[at] = value[at * each : (at + 1) * each]
    for k in range(n_gy):
        for j in range(n_gz):
            outs[k][j] = total[lax.rem(where[1] + k, n_gy) * n_gz + j].astype(BF16)


def attend_body(n_gy, n_gz, *refs):
    where = position()
    lengths, pieces, rest = refs[:n_gz], refs[n_gz : n_gz + n_gy], refs[n_gz + n_gy :]
    keys, values = rest[:n_gz], rest[n_gz : 2 * n_gz]
    outs, held, given = rest[2 * n_gz : -2], rest[-2], rest[-1]
    each, width = pieces[0].shape[1:]
    heads = width // HDIM
    lines = n_gy * heads
    half = held.shape[-1]
    halves = range(HDIM // half)
    sources = [lax.rem(where[2] + n_gz - j, n_gz) for j in range(n_gz)]
    for j in range(n_gz):
        for k in range(n_gy):
            mine = pieces[k][sources[j]].astype(F32)
            for h in range(heads):
                line = (k * heads + h) * each
                for p in halves:
                    at = h * HDIM + p * half
                    held[j, p, line : line + each, :] = mine[:, at : at + half]
    rows = [(j, r) for j in range(n_gz) for r in range(each)]
    scores = []
    for j, r in rows:
        span = pl.ds(r, lines, stride=each)
        query = jnp.concatenate([held[j, p, span, :] for p in halves], axis=1).astype(BF16)
        score = lax.dot_general(query, keys[j][r], (((1,), (1,)), ((), ())), preferred_element_type=F32)
        place = lax.broadcasted_iota(jnp.int32, score.shape, 1)
        scores.append(jnp.where(place < lengths[j][r], score * HDIM ** (-0.5), -jnp.inf))
    raised = [jnp.exp(score - jnp.max(score, axis=1, keepdims=True)) for score in scores]
    totals = [jnp.sum(weight, axis=1, keepdims=True) for weight in raised]
    for (j, r), weight, total in zip(rows, raised, totals):
        mixed = jnp.dot(weight.astype(BF16), values[j][r], preferred_element_type=F32) / total
        for p in halves:
            given[j, p, pl.ds(r, lines, stride=each), :] = mixed[:, p * half : (p + 1) * half]
    for j in range(n_gz):
        for k in range(n_gy):
            for h in range(heads):
                line = ((n_gy - k) % n_gy * heads + h) * each
                for p in halves:
                    at = h * HDIM + p * half
                    outs[k][sources[j], :, at : at + half] = given[j, p, line : line + each, :].astype(BF16)


def gather_rows_body(n_gy, n_gz, *refs):
    where = position()
    pieces, outs, total = refs[:n_gy], refs[n_gy:-1], refs[-1]
    for k in range(n_gy):
        for j in range(n_gz):
            total[lax.rem(where[1] + n_gy - k, n_gy) * n_gz + j] = pieces[k][j].astype(F32)
    value = jnp.concatenate([total[i] for i in range(n_gy * n_gz)], axis=0).astype(BF16)
    for out in outs:
        out[...] = value


def output_body(n_gx, n_gy, n_gz, chunk, first, *refs):
    where = position()
    pieces, weight = refs[:n_gx], refs[n_gx]
    count = n_gy * n_gz
    outs = refs[n_gx + 1 : n_gx + 1 + count]
    rows, total = refs[n_gx + 1 + count :]
    block = pieces[0].shape[0]
    for k in range(n_gx):
        at = pl.multiple_of(lax.rem(where[0] + n_gx - k, n_gx) * block, block)
        rows[pl.ds(at, block), :] = pieces[k][...]
    part = outs[0].shape[0]
    count = block * n_gx
    clear_below(rows, count)
    for c in range(outs[0].shape[1] // chunk):
        span = slice(first + c * chunk, first + (c + 1) * chunk)
        total[...] = product(rows, weight, span, 768)[:count]
        for k in range(n_gy):
            for j in range(n_gz):
                at = lax.rem(where[1] + k, n_gy) * n_gz + lax.rem(where[2] + j, n_gz)
                at = pl.multiple_of(at * part, part)
                outs[k * n_gz + j][:, c * chunk : (c + 1) * chunk] = total[pl.ds(at, part), :].astype(BF16)


def sum_body(*refs):
    value = refs[0][...].astype(F32)
    for ref in refs[1:-1]:
        value = value + ref[...].astype(F32)
    refs[-1][...] = value.astype(BF16)


def sum_parts_body(*refs):
    pieces, out = refs[:-1], refs[-1]
    wide = pieces[0].shape[1]
    each = len(pieces) // (out.shape[1] // wide)
    for c in range(out.shape[1] // wide):
        value = pieces[c * each][...].astype(F32)
        for piece in pieces[c * each + 1 : (c + 1) * each]:
            value = value + piece[...].astype(F32)
        out[:, c * wide : (c + 1) * wide] = value.astype(BF16)


def added(arrays, name):
    out = jax.ShapeDtypeStruct(arrays[0].shape, BF16)
    return call(sum_body, [out], arrays, [VMEM] * len(arrays), name=name)[0]


def mib_for(*sizes):
    return max(8, -(-int(sum(sizes) * 1.25) // 2**20) + 2)


def shards(tokens, q_weight, o_weight, key_cache, value_cache, lengths):
    n_gx, n_gy, n_gz = (lax.axis_size(a) for a in ("gx", "gy", "gz"))
    own_rows, depth = tokens.shape
    row_count = own_rows * n_gy * n_gz
    width = q_weight.shape[1]
    each = key_cache.shape[0]
    tall = max(row_count, 128)
    part = row_count // n_gx
    struct = jax.ShapeDtypeStruct

    weight_bytes = 2 * depth * width
    staged = call(
        stage_body,
        [struct(tokens.shape, BF16)],
        [tokens],
        [ANY],
        scratch=[pltpu.SemaphoreType.DMA],
        beside=3000 * weight_bytes,
        name="own_tokens",
    )[0]
    pieces = []
    for k in range(n_gy):
        over = shift(tokens, "gy", k) if k else tokens
        pieces += [shift(over, "gz", j) if j else over for j in range(n_gz)]
    pieces[0] = staged
    chip_keys, chip_values, chip_lengths = (
        [array] + [shift(array, "gz", j) for j in range(1, n_gz)] for array in (key_cache, value_cache, lengths)
    )
    pieces, chip_keys, chip_values, chip_lengths = lax.optimization_barrier(
        (pieces, chip_keys, chip_values, chip_lengths)
    )
    chunk = largest_divisor(width, 256, 128)
    terms = call(
        functools.partial(query_body, n_gx, n_gy, n_gz, chunk),
        [struct((part, width), BF16)] * n_gx,
        [*pieces, q_weight],
        [VMEM] * len(pieces) + [VMEM],
        scratch=[
            pltpu.VMEM((tall, depth), BF16),
            pltpu.VMEM((row_count, width), F32),
        ],
        mib=mib_for(tall * depth * 4, tall * width * 8, depth * width * 2),
        flops=2 * row_count * depth * width,
        name="query_terms",
    )

    terms = [terms[0]] + [shift(terms[k], "gx", k) for k in range(1, n_gx)]
    queries = call(
        functools.partial(sum_split_body, n_gx, n_gy, n_gz),
        [struct((n_gz, each, width), BF16)] * n_gy,
        [*terms],
        [VMEM] * n_gx,
        scratch=[pltpu.VMEM((n_gy * n_gz, each, width), F32)],
        beside=20000 * key_cache.size,
        name="query_sum",
    )
    pieces = hops(queries, "gy")
    mixed = call(
        functools.partial(attend_body, n_gy, n_gz),
        [struct((n_gz, each, width), BF16)] * n_gy,
        [*chip_lengths, *pieces, *chip_keys, *chip_values],
        [SMEM] * n_gz + [VMEM] * (n_gy + 2 * n_gz),
        scratch=[pltpu.VMEM((n_gz, HDIM // 128, n_gy * width // HDIM * each, 128), F32)] * 2,
        mib=12,
        name="attention",
    )

    pieces = hops(mixed, "gy")
    copies = call(
        functools.partial(gather_rows_body, n_gy, n_gz),
        [struct((part, width), BF16)] * n_gx,
        pieces,
        [VMEM] * n_gy,
        scratch=[pltpu.VMEM((n_gy * n_gz, each, width), F32)],
        name="mixed_rows",
    )
    blocks = [copies[0]] + [shift(copies[k], "gx", k) for k in range(1, n_gx)]
    columns = o_weight.shape[1]
    splits = 2 if columns % 512 == 0 else 1
    wide = columns // splits
    chunk = largest_divisor(wide, 768, 128)
    terms = [
        call(
            functools.partial(output_body, n_gx, n_gy, n_gz, chunk, c * wide),
            [struct((own_rows, wide), BF16)] * (n_gy * n_gz),
            [*blocks, o_weight],
            [VMEM] * (n_gx + 1),
            scratch=[pltpu.VMEM((tall, width), BF16), pltpu.VMEM((row_count, chunk), F32)],
            mib=mib_for(tall * width * 4, tall * (chunk * 4 + wide * 2), columns * width * 2),
            flops=2 * tall * wide * width,
            name="output_terms",
        )
        for c in range(splits)
    ]

    leaving, arrived = [], []
    for term in terms:
        for k in range(1, n_gy):
            mine = [term[k * n_gz + (j + across()) % n_gz] for j in range(n_gz)]
            mine = [mine[0]] + [shift(mine[j], "gz", j) for j in range(1, n_gz)]
            leaving.append(added(mine, "pair_sum") if n_gz > 1 else mine[0])
    for at, array in enumerate(leaving):
        arrived.append(hop(array, "gy", at % (n_gy - 1) + 1))
    staying = [term[j] for term in terms for j in range(1, n_gz)]
    if leaving and staying:
        leaving, staying = lax.optimization_barrier((leaving, staying))
    operands = []
    for c, term in enumerate(terms):
        operands.append(term[0])
        operands += [shift(staying[c * (n_gz - 1) + j - 1], "gz", j) for j in range(1, n_gz)]
        operands += arrived[c * (n_gy - 1) : (c + 1) * (n_gy - 1)]
    return call(
        sum_parts_body,
        [struct((own_rows, columns), BF16)],
        operands,
        [VMEM] * len(operands),
        name="output_sum",
    )[0]


def solution(mesh):
    return jax.shard_map(
        shards,
        mesh=mesh,
        in_specs=(
            P(("groups", "gy", "gz"), "gx"),
            P("gx", ("gy", "gz")),
            P(("gy", "gz"), "gx"),
            P(("groups", "gx", "gy", "gz"), None, None),
            P(("groups", "gx", "gy", "gz"), None, None),
            P(("groups", "gx", "gy", "gz")),
        ),
        out_specs=P(("groups", "gy", "gz"), "gx"),
        check_vma=False,
    )
```
